128 devices in a mesh: vel: 4 (over y_lo, core), pos: 32 (over y_hi, z, x).
Axes of the slice: x: 4, y: 4 (y_hi: 2, y_lo: 2; y = y_hi * 2 + y_lo), z: 4, core: 2. Of those that a mesh axis runs over, the one named last changes fastest.
Arguments:
- value_next: float32 [64, 64, 64, 512], P('pos', 'vel'), may hold values from -6 to 6
- density: float32 [64, 64, 64, 512], P('pos', 'vel'), as said below
Outputs:
- value_now: float32 [64, 64, 64, 512], P('pos', 'vel')
- density_next: float32 [64, 64, 64, 512], P('pos', 'vel')
The draws below stay inside these ranges and needn't reach their ends.
Inputs may be any that keep to these rules, and one draw needn't show every extreme that they name: density is positive everywhere.
All inputs are finite; a program needn't handle non-finite values.
Results may differ from the reference program's by a relative error of at most 0.00002.
Values sent between devices are 32-bit elements; how exact they have to be, the bound alone decides.
A program may use at most 192 MiB of HBM per device.

```python
import math
import jax
import jax.numpy as jnp
from jax import lax

NV = 64
NY = 512
NX = 64


def draw_density(key, part):
    first, second, third = jax.random.split(key, 3)
    rising = 10.0 ** (jnp.arange(NV, dtype=jnp.float32) / (NV - 1))
    column_scale = jnp.exp(jax.random.uniform(first, (NV,), jnp.float32, 0.0, math.log(10.0)))
    noise = jax.random.uniform(second, (NX, NV, NV, NY), jnp.float32, 0.5, 1.5)
    place = jnp.exp(jax.random.uniform(third, (NX, NY), jnp.float32, math.log(0.3), math.log(3.0)))
    result = place[:, None, None, :] * rising[None, :, None, None] * column_scale[None, None, :, None] * noise / 15.0
    return result.astype(jnp.float32)


def block_scale(key, extent, cuts, smallest, high):
    level = 1.0
    for axis_at, blocks in cuts:
        heights = jax.random.uniform(jax.random.fold_in(jax.random.fold_in(key, 6), axis_at), (blocks,), jnp.float32, smallest / len(cuts), high / len(cuts))
        level = level * jnp.repeat(jnp.exp(heights), extent[axis_at] // blocks).reshape((-1,) + (1,) * (len(extent) - 1 - axis_at))
    return level


def bell_draw(rng, dims, width, limit, cuts=(), kind=jnp.bfloat16):
    values = width * jax.random.normal(rng, dims, jnp.float32)
    if cuts:
        values = values * block_scale(rng, dims, cuts, -0.22, 0.18)
    return jnp.clip(values, -limit, limit).astype(kind)


def setup_inputs(seed: int = 0) -> dict:
    streams_of = jax.random.split(jax.random.key(seed), 3)
    value_next = bell_draw(streams_of[0], (NX, NV, NV, NY), 1.0, 6.0, ((0, 32), (1, 4)), jnp.float32)
    density = draw_density(jax.random.fold_in(streams_of[2], 71), 0)
    return {"value_next": value_next, "density": density}


COURANT = 0.4
CONTROL_COST = 0.25
VISCOSITY = 0.15
CROWDING = 0.3


def speeds(first, count, total):
    index = first + jnp.arange(count, dtype=jnp.int32)
    return COURANT * ((index.astype(jnp.float32) + 0.5 - total / 2) / (total / 2))


def along_second(array, step):
    rolled = jnp.roll(array, -step, 2)
    place = lax.broadcasted_iota(jnp.int32, array.shape, 2)
    edge = array.shape[2] - 1 if step > 0 else 0
    return jnp.where(place == edge, array, rolled)


def value_core(centre, x_up, x_dn, a_up, a_dn, speed_x, speed_y, crowding):
    along_x = speed_x[None, :, None, None]
    along_y = speed_y[None, None, :, None]
    carry_x = jnp.where(along_x > 0, along_x * (x_up - centre), along_x * (centre - x_dn))
    ahead_y = jnp.roll(centre, -1, 3) - centre
    behind_y = centre - jnp.roll(centre, 1, 3)
    carry_y = jnp.where(along_y > 0, along_y * ahead_y, along_y * behind_y)
    upper_v = a_up - centre
    lower_v = centre - a_dn
    upper_w = along_second(centre, 1) - centre
    lower_w = centre - along_second(centre, -1)
    hamilton = 0.5 * (jnp.square(jnp.maximum(lower_v, 0.0)) + jnp.square(jnp.minimum(upper_v, 0.0))
                      + jnp.square(jnp.maximum(lower_w, 0.0)) + jnp.square(jnp.minimum(upper_w, 0.0)))
    laplace = upper_v - lower_v + upper_w - lower_w
    return centre + carry_x + carry_y - CONTROL_COST * hamilton + VISCOSITY * laplace + crowding[:, None, None, :]


def density_core(centre, x_up, x_dn, a_up, a_dn, control, control_up, control_dn, speed_x, speed_y):
    along_x = speed_x[None, :, None, None]
    along_y = speed_y[None, None, :, None]
    carry_x = jnp.where(along_x > 0, along_x * (centre - x_dn), along_x * (x_up - centre))
    behind_y = centre - jnp.roll(centre, 1, 3)
    ahead_y = jnp.roll(centre, -1, 3) - centre
    carry_y = jnp.where(along_y > 0, along_y * behind_y, along_y * ahead_y)
    speed_up = -CONTROL_COST * (control_up - control)
    speed_dn = -CONTROL_COST * (control - control_dn)
    flux_up = jnp.maximum(speed_up, 0.0) * centre + jnp.minimum(speed_up, 0.0) * a_up
    flux_dn = jnp.maximum(speed_dn, 0.0) * a_dn + jnp.minimum(speed_dn, 0.0) * centre
    b_up = along_second(centre, 1)
    b_dn = along_second(centre, -1)
    side_up = -CONTROL_COST * (along_second(control, 1) - control)
    side_dn = -CONTROL_COST * (control - along_second(control, -1))
    flux_right = jnp.maximum(side_up, 0.0) * centre + jnp.minimum(side_up, 0.0) * b_up
    flux_left = jnp.maximum(side_dn, 0.0) * b_dn + jnp.minimum(side_dn, 0.0) * centre
    spread = VISCOSITY * (a_up + a_dn - 2.0 * centre + b_up + b_dn - 2.0 * centre)
    return centre - carry_x - carry_y - (flux_up - flux_dn) - (flux_right - flux_left) + spread


def reference(value_next, density):
    grid_v = value_next.shape[1]
    mass = jnp.sum(density, axis=(1, 2)) / (grid_v * grid_v)
    crowding = CROWDING * mass * mass
    speed_all = speeds(0, grid_v, grid_v)
    pieces = []
    for offset in range(0, grid_v, 8):
        rows = offset + jnp.arange(8, dtype=jnp.int32)
        upper = jnp.minimum(rows + 1, grid_v - 1).astype(jnp.int32)
        lower = jnp.maximum(rows - 1, 0).astype(jnp.int32)
        centre = value_next[:, offset:offset + 8]
        pieces.append(value_core(centre, jnp.roll(centre, -1, 0), jnp.roll(centre, 1, 0),
                                 jnp.take(value_next, upper, axis=1), jnp.take(value_next, lower, axis=1),
                                 speed_all[offset:offset + 8], speed_all, crowding))
    value_now = jnp.concatenate(pieces, 1)
    parts = []
    for offset in range(0, grid_v, 8):
        rows = offset + jnp.arange(8, dtype=jnp.int32)
        upper = jnp.minimum(rows + 1, grid_v - 1).astype(jnp.int32)
        lower = jnp.maximum(rows - 1, 0).astype(jnp.int32)
        centre = density[:, offset:offset + 8]
        parts.append(density_core(centre, jnp.roll(centre, -1, 0), jnp.roll(centre, 1, 0),
                                  jnp.take(density, upper, axis=1), jnp.take(density, lower, axis=1),
                                  value_now[:, offset:offset + 8], jnp.take(value_now, upper, axis=1),
                                  jnp.take(value_now, lower, axis=1), speed_all[offset:offset + 8], speed_all))
    density_next = jnp.concatenate(parts, 1)
    return value_now, density_next
```

```python
import functools

import jax
import jax.numpy as jnp
from jax import lax
from jax.experimental import pallas as pl
from jax.experimental.pallas import tpu as pltpu
from jax.sharding import PartitionSpec as P

MESH = pl.DeviceIdType.MESH
COURANT = 0.4
CROWDING = 0.3
ROWS = 16
GRID_V = 64
NY = 512
TILE = 8
TILES = GRID_V // TILE
VEL = 4
POS = 32
F32 = jnp.float32
PASSED = range(1, 8)


def tile(t):
    return pl.ds(t * TILE, TILE)


def sublane():
    return lax.broadcasted_iota(jnp.int32, (TILE, NY), 0)


def speed_b(t):
    index = (sublane() + t * TILE).astype(F32)
    return jnp.abs(COURANT * ((index + 0.5 - GRID_V / 2) / (GRID_V / 2)))


def value_slab(c_ref, up_ref, dn_ref, x_ref, crowd, speed_x, out_ref):
    place = sublane()
    c = c_ref[tile(0), :]
    turned = pltpu.roll(c, TILE - 1, 0)
    carried = jnp.zeros((TILE, NY), F32)
    for t in range(TILES):
        if t + 1 < TILES:
            c_next = c_ref[tile(t + 1), :]
            turned_next = pltpu.roll(c_next, TILE - 1, 0)
        else:
            c_next, turned_next = None, c
        upper = jnp.where(place == TILE - 1, turned_next, turned) - c
        gain = upper * (1.2 - jnp.minimum(upper, 0.0))
        loss = pltpu.roll(upper * (1.2 + jnp.maximum(upper, 0.0)), 1, 0)
        gain = gain - jnp.where(place == 0, carried, loss)
        carried = loss
        a_upper = up_ref[tile(t), :] - c
        a_lower = c - dn_ref[tile(t), :]
        gain = gain + a_upper * (1.2 - jnp.minimum(a_upper, 0.0))
        gain = gain - a_lower * (1.2 + jnp.maximum(a_lower, 0.0))
        y_next = pltpu.roll(c, 1 if t < TILES // 2 else NY - 1, 1)
        speed_y = speed_b(t)
        out = (1.0 - speed_x - speed_y) * c + speed_x * x_ref[tile(t), :] + speed_y * y_next
        out_ref[tile(t), :] = out + (0.125 * gain + crowd)
        c, turned = c_next, turned_next


def density_slab(n_ref, n_up_ref, n_dn_ref, d_ref, d_up_ref, d_dn_ref, x_ref, speed_x, out_ref):
    place = sublane()
    d, n = d_ref[tile(0), :], n_ref[tile(0), :]
    d_turned, n_turned = pltpu.roll(d, TILE - 1, 0), pltpu.roll(n, TILE - 1, 0)
    carried = jnp.zeros((TILE, NY), F32)
    for t in range(TILES):
        if t + 1 < TILES:
            d_next, n_next = d_ref[tile(t + 1), :], n_ref[tile(t + 1), :]
            d_turned_next = pltpu.roll(d_next, TILE - 1, 0)
            n_turned_next = pltpu.roll(n_next, TILE - 1, 0)
        else:
            d_next, n_next, d_turned_next, n_turned_next = None, None, d, n
        last = place == TILE - 1
        d_beyond = jnp.where(last, d_turned_next, d_turned)
        step = n - jnp.where(last, n_turned_next, n_turned)
        flux = (jnp.maximum(step, 0.0) + 0.6) * (d - d_beyond) + step * d_beyond
        turned = pltpu.roll(flux, 1, 0)
        total = jnp.where(place == 0, carried, turned) - flux
        carried = turned
        d_up, d_dn = d_up_ref[tile(t), :], d_dn_ref[tile(t), :]
        step = n - n_up_ref[tile(t), :]
        total = total - ((jnp.maximum(step, 0.0) + 0.6) * (d - d_up) + step * d_up)
        step = n_dn_ref[tile(t), :] - n
        total = total + ((jnp.maximum(step, 0.0) + 0.6) * (d_dn - d) + step * d)
        y_next = pltpu.roll(d, NY - 1 if t < TILES // 2 else 1, 1)
        speed_y = speed_b(t)
        out = (1.0 - speed_x - speed_y) * d + speed_y * y_next
        if x_ref is not None:
            out = out + speed_x * x_ref[tile(t), :]
        out_ref[tile(t), :] = out + 0.25 * total
        d, n, d_turned, n_turned = d_next, n_next, d_turned_next, n_turned_next


def kernel(
    value, density, value_out, density_out,
    v, d, hv, hd, n, dn, mass, crowd, passing,
    load_sem, edge_send, edge_recv, mass_send, mass_recv, x_send, x_recv, pass_send, pass_recv, out_sem,
):
    vel, pos = lax.axis_index("vel"), lax.axis_index("pos")
    above, below = lax.rem(pos + 1, POS), lax.rem(pos + POS - 1, POS)
    low = vel < VEL // 2
    value_to = jnp.where(low, above, below)
    density_to = jnp.where(low, below, above)
    near = jnp.where(low, 0, 1)
    far = 1 - near
    has_lower, has_upper = vel > 0, vel < VEL - 1
    half = POS // 2
    place_x = lax.rem(pos, half)
    bottom, top = place_x == 0, place_x == half - 1
    at_end = jnp.logical_or(bottom, top)
    twin = lax.rem(pos + half, POS)
    other_end = jnp.where(bottom, pos + half - 1, pos - half + 1)
    high = jnp.logical_not(low)
    value_long = jnp.logical_or(jnp.logical_and(top, low), jnp.logical_and(bottom, high))
    density_long = jnp.logical_and(at_end, jnp.logical_not(value_long))

    barrier = pltpu.get_barrier_semaphore()
    for other in (above, below):
        pl.semaphore_signal(barrier, inc=1, device_id={"pos": other}, device_id_type=MESH)
    for k in range(1, VEL):
        pl.semaphore_signal(barrier, inc=1, device_id={"vel": lax.rem(vel + k, VEL)}, device_id_type=MESH)

    @pl.when(at_end)
    def _():
        pl.semaphore_signal(barrier, inc=1, device_id={"pos": twin}, device_id_type=MESH)
        pl.semaphore_signal(barrier, inc=1, device_id={"pos": other_end}, device_id_type=MESH)

    load_d = pltpu.make_async_copy(density, d.at[:, pl.ds(1, ROWS)], load_sem.at[0])
    load_v = pltpu.make_async_copy(value, v.at[:, pl.ds(1, ROWS)], load_sem.at[1])
    load_d.start()
    load_v.start()
    pl.semaphore_wait(barrier, jnp.where(at_end, 2 + VEL - 1 + 2, 2 + VEL - 1))

    def x_copies(a):
        one = pl.ds(a, 1)
        return (
            pltpu.make_async_remote_copy(
                value.at[far, one], hv.at[one], x_send.at[0, a], x_recv.at[0, a],
                device_id={"pos": value_to}, device_id_type=MESH),
            pltpu.make_async_remote_copy(
                density.at[near, one], hd.at[one], x_send.at[1, a], x_recv.at[1, a],
                device_id={"pos": density_to}, device_id_type=MESH),
        )

    def start_x(a):
        for copy in x_copies(a):
            copy.start()

    def start_x_passed(a):
        one, k = pl.ds(a, 1), a - PASSED[0]
        for kind, (copy, source, row, crosses) in enumerate(
            zip(x_copies(a), (value, density), (far, near), (value_long, density_long))
        ):
            first_leg = pltpu.make_async_remote_copy(
                source.at[row, one], passing.at[pl.ds(k, 1)], x_send.at[kind, a], pass_recv.at[k],
                device_id={"pos": other_end}, device_id_type=MESH)
            pl.when(crosses)(first_leg.start)
            pl.when(jnp.logical_not(crosses))(copy.start)

    def second_legs(a):
        one, k = pl.ds(a, 1), a - PASSED[0]
        return [
            pltpu.make_async_remote_copy(
                passing.at[pl.ds(k, 1)], halo.at[one], pass_send.at[k], x_recv.at[kind, a],
                device_id={"pos": twin}, device_id_type=MESH)
            for kind, halo in enumerate((hv, hd))
        ]

    def pass_on(a):
        @pl.when(at_end)
        def _():
            value_leg, density_leg = second_legs(a)
            k = a - PASSED[0]
            first_leg = pltpu.make_async_remote_copy(
                value.at[far, pl.ds(a, 1)], passing.at[pl.ds(k, 1)], x_send.at[0, a], pass_recv.at[k],
                device_id={"pos": other_end}, device_id_type=MESH)
            first_leg.wait_recv()
            pl.when(density_long)(value_leg.start)
            pl.when(value_long)(density_leg.start)

    def edge_copies(k, source, target):
        to_upper = pltpu.make_async_remote_copy(
            source.at[:, pl.ds(ROWS - 1, 1)], target.at[:, pl.ds(0, 1)], edge_send.at[k, 0], edge_recv.at[k, 0],
            device_id={"vel": lax.rem(vel + 1, VEL)}, device_id_type=MESH)
        to_lower = pltpu.make_async_remote_copy(
            source.at[:, pl.ds(0, 1)], target.at[:, pl.ds(ROWS + 1, 1)], edge_send.at[k, 1], edge_recv.at[k, 1],
            device_id={"vel": lax.rem(vel + VEL - 1, VEL)}, device_id_type=MESH)
        return to_upper, to_lower

    def start_pair(pair):
        to_upper, to_lower = pair

        @pl.when(has_upper)
        def _():
            to_upper.start()

        @pl.when(has_lower)
        def _():
            to_lower.start()

    def receive_pair(pair):
        to_upper, to_lower = pair

        @pl.when(has_lower)
        def _():
            to_upper.wait_recv()

        @pl.when(has_upper)
        def _():
            to_lower.wait_recv()

    def sent_pair(pair):
        to_upper, to_lower = pair

        @pl.when(has_upper)
        def _():
            to_upper.wait_send()

        @pl.when(has_lower)
        def _():
            to_lower.wait_send()

    edges_v, edges_d = edge_copies(0, value, v), edge_copies(1, density, d)
    start_x(0)
    start_pair(edges_v)
    start_x(ROWS - 1)
    start_pair(edges_d)
    for a in range(1, ROWS - 1):
        (start_x_passed if a in PASSED else start_x)(a)

    load_d.wait()
    place = sublane()

    def add_row(i, sums):
        parts = []
        for r in range(2):
            total = sums[r]
            for t in range(TILES):
                total = total + d[r, i + 1, tile(t), :]
            parts.append(total)
        return tuple(parts)

    zero = jnp.zeros((TILE, NY), F32)
    sums = lax.fori_loop(0, ROWS, add_row, (zero, zero))
    sums = [jnp.sum(s, axis=0, keepdims=True) for s in sums]
    mass[vel] = jnp.where(place == 0, sums[0], sums[1])
    mass_copies = [
        pltpu.make_async_remote_copy(
            mass.at[vel], mass.at[vel], mass_send.at[k], mass_recv.at[k],
            device_id={"vel": lax.rem(vel + k, VEL)}, device_id_type=MESH)
        for k in range(1, VEL)
    ]
    for copy in mass_copies:
        copy.start()
    load_v.wait()

    def repeat_edges(field, rows):
        @pl.when(jnp.logical_not(has_lower))
        def _():
            for r in rows:
                field[r, 0] = field[r, 1]

        @pl.when(jnp.logical_not(has_upper))
        def _():
            for r in rows:
                field[r, ROWS + 1] = field[r, ROWS]

    repeat_edges(v, (0, 1))
    repeat_edges(d, (0, 1))
    for copy in mass_copies:
        copy.wait_recv()
    total = (mass[0] + mass[1]) + (mass[2] + mass[3])
    total = total / (GRID_V * GRID_V)
    total = CROWDING * total * total
    crowd[0] = jnp.broadcast_to(total[0:1], (TILE, NY))
    crowd[1] = jnp.broadcast_to(total[1:2], (TILE, NY))

    def speed_a(a):
        index = (vel * ROWS + a).astype(F32)
        return jnp.abs(COURANT * ((index + 0.5 - GRID_V / 2) / (GRID_V / 2)))

    def value_row(row, a, x_ref):
        value_slab(v.at[row, a + 1], v.at[row, a + 2], v.at[row, a], x_ref, crowd[row], speed_a(a), n.at[row, a + 1])

    def density_row(row, a, x_ref, out_ref):
        density_slab(
            n.at[row, a + 1], n.at[row, a + 2], n.at[row, a],
            d.at[row, a + 1], d.at[row, a + 2], d.at[row, a], x_ref, speed_a(a), out_ref)

    def write(k, row, a):
        source, target = ((n, value_out), (dn, density_out))[k]
        at = a + 1 if k == 0 else a
        return pltpu.make_async_copy(source.at[row, pl.ds(at, 1)], target.at[row, pl.ds(a, 1)], out_sem.at[k])

    def arrive(a):
        for copy in x_copies(a):
            copy.wait_recv()

    def finish_far(a):
        speed_x = speed_a(a)
        for t in range(TILES):
            dn[far, a, tile(t), :] = dn[far, a, tile(t), :] + speed_x * hd[a, tile(t), :]
        write(1, far, a).start()

    def near_density(a):
        density_row(near, a, d.at[far, a + 1], dn.at[near, a])
        write(1, near, a).start()

    @pl.loop(1, ROWS - 1)
    def _(a):
        value_row(far, a, v.at[near, a + 1])
        write(0, far, a).start()

    receive_pair(edges_v)

    @pl.loop(0, 2)
    def _(i):
        a = i * (ROWS - 1)
        arrive(a)
        value_row(far, a, v.at[near, a + 1])
        value_row(near, a, hv.at[a])
        write(0, far, a).start()
        write(0, near, a).start()

    edges_n = edge_copies(2, n.at[:, pl.ds(1, ROWS)], n)
    start_pair(edges_n)
    repeat_edges(n, (0, 1))

    @pl.loop(1, ROWS - 1)
    def _(a):
        density_row(far, a, None, dn.at[far, a])

    receive_pair(edges_d)

    pass_on(1)
    pass_on(2)
    pass_on(3)

    def near_step(a):
        arrive(a)
        value_row(near, a, hv.at[a])
        write(0, near, a).start()
        finish_far(a)

    @pl.loop(1, ROWS // 2)
    def _(a):
        pl.when(a + 3 < ROWS // 2)(lambda: pass_on(a + 3))
        near_step(a)

        @pl.when(a > 1)
        def _():
            near_density(a - 1)

    receive_pair(edges_n)

    @pl.loop(0, 2)
    def _(i):
        a = i * (ROWS - 1)
        density_row(far, a, None, dn.at[far, a])
        finish_far(a)

    near_density(0)

    @pl.loop(ROWS // 2, ROWS - 1)
    def _(a):
        near_step(a)
        near_density(a - 1)

    near_density(ROWS - 2)
    near_density(ROWS - 1)

    for pair in (edges_v, edges_d, edges_n):
        sent_pair(pair)
    for copy in mass_copies:
        copy.wait_send()

    @pl.loop(0, ROWS)
    def _(a):
        for copy in x_copies(a):
            copy.wait_send()

    @pl.when(at_end)
    def _():
        for a in PASSED:
            second_legs(a)[0].wait_send()

    pltpu.make_async_copy(n.at[:, pl.ds(1, ROWS)], value_out, out_sem.at[0]).wait()
    pltpu.make_async_copy(dn, density_out, out_sem.at[1]).wait()


def body(value_next, density):
    shape = (2, ROWS, GRID_V, NY)
    haloed = pltpu.VMEM((2, ROWS + 2, GRID_V, NY), F32)
    slab = pltpu.VMEM((ROWS, GRID_V, NY), F32)
    dma = pltpu.SemaphoreType.DMA
    return pl.pallas_call(
        kernel,
        out_shape=[jax.ShapeDtypeStruct(shape, F32)] * 2,
        in_specs=[pl.BlockSpec(memory_space=pl.ANY)] * 2,
        out_specs=[pl.BlockSpec(memory_space=pl.ANY)] * 2,
        scratch_shapes=[
            haloed, haloed, slab, slab, haloed, pltpu.VMEM(shape, F32),
            pltpu.VMEM((VEL, TILE, NY), F32), pltpu.VMEM((2, TILE, NY), F32),
            pltpu.VMEM((len(PASSED), GRID_V, NY), F32),
            dma((2,)), dma((3, 2)), dma((3, 2)), dma((VEL,)), dma((VEL,)),
            dma((2, ROWS)), dma((2, ROWS)), dma((len(PASSED),)), dma((len(PASSED),)), dma((2,)),
        ],
        compiler_params=pltpu.CompilerParams(
            collective_id=0, has_side_effects=True, vmem_limit_bytes=48 << 20
        ),
    )(value_next, density)


def solution(mesh):
    spec = P("pos", "vel", None, None)
    return jax.shard_map(body, mesh=mesh, in_specs=(spec, spec), out_specs=(spec, spec), check_vma=False)
```

```python
import functools

import jax
import jax.numpy as jnp
from jax import lax
from jax.experimental import pallas as pl
from jax.experimental.pallas import tpu as pltpu
from jax.sharding import PartitionSpec as P

MESH = pl.DeviceIdType.MESH
COURANT = 0.4
CROWDING = 0.3
ROWS = 16
GRID_V = 64
NY = 512
TILE = 8
TILES = GRID_V // TILE
VEL = 4
POS = 32
F32 = jnp.float32
PASSED = range(1, 7)

LAST = ROWS - 2
ORDER = (1, 2, 3, 0, ROWS - 1, *range(4, ROWS - 1))


def tile(t):
    return pl.ds(t * TILE, TILE)


def sublane():
    return lax.broadcasted_iota(jnp.int32, (TILE, NY), 0)


def speed_b(t):
    index = (sublane() + t * TILE).astype(F32)
    return jnp.abs(COURANT * ((index + 0.5 - GRID_V / 2) / (GRID_V / 2)))


def value_slab(c_ref, up_ref, dn_ref, x_ref, crowd, speed_x, out_ref, first=0, stop=TILES):
    place = sublane()

    def ahead(t):
        c = c_ref[tile(t), :]
        return c, pltpu.roll(c, TILE - 1, 0)

    begin = max(first - 1, 0)
    c, turned = ahead(begin)
    carried = jnp.zeros((TILE, NY), F32)
    for t in range(begin, stop):
        c_next, turned_next = ahead(t + 1) if t + 1 < TILES else (None, c)
        upper = jnp.where(place == TILE - 1, turned_next, turned) - c
        loss = pltpu.roll(upper * (1.2 + jnp.maximum(upper, 0.0)), 1, 0)
        if t >= first:
            gain = upper * (1.2 - jnp.minimum(upper, 0.0)) - jnp.where(place == 0, carried, loss)
            a_upper = up_ref[tile(t), :] - c
            a_lower = c - dn_ref[tile(t), :]
            gain = gain + a_upper * (1.2 - jnp.minimum(a_upper, 0.0))
            gain = gain - a_lower * (1.2 + jnp.maximum(a_lower, 0.0))
            y_next = pltpu.roll(c, 1 if t < TILES // 2 else NY - 1, 1)
            speed_y = speed_b(t)
            out = (1.0 - speed_x - speed_y) * c + speed_x * x_ref[tile(t), :] + speed_y * y_next
            out_ref[tile(t), :] = out + (0.125 * gain + crowd)
        carried = loss
        c, turned = c_next, turned_next


def density_slab(n_ref, n_up_ref, n_dn_ref, d_ref, d_up_ref, d_dn_ref, x_ref, speed_x, out_ref, first=0, stop=TILES):
    place = sublane()

    def ahead(t):
        d, n = d_ref[tile(t), :], n_ref[tile(t), :]
        return d, n, pltpu.roll(d, TILE - 1, 0), pltpu.roll(n, TILE - 1, 0)

    begin = max(first - 1, 0)
    d, n, d_turned, n_turned = ahead(begin)
    carried = jnp.zeros((TILE, NY), F32)
    for t in range(begin, stop):
        d_next, n_next, d_turned_next, n_turned_next = ahead(t + 1) if t + 1 < TILES else (None, None, d, n)
        last = place == TILE - 1
        d_beyond = jnp.where(last, d_turned_next, d_turned)
        step = n - jnp.where(last, n_turned_next, n_turned)
        flux = (jnp.maximum(step, 0.0) + 0.6) * (d - d_beyond) + step * d_beyond
        turned = pltpu.roll(flux, 1, 0)
        if t >= first:
            total = jnp.where(place == 0, carried, turned) - flux
            d_up, d_dn = d_up_ref[tile(t), :], d_dn_ref[tile(t), :]
            step = n - n_up_ref[tile(t), :]
            total = total - ((jnp.maximum(step, 0.0) + 0.6) * (d - d_up) + step * d_up)
            step = n_dn_ref[tile(t), :] - n
            total = total + ((jnp.maximum(step, 0.0) + 0.6) * (d_dn - d) + step * d)
            y_next = pltpu.roll(d, NY - 1 if t < TILES // 2 else 1, 1)
            speed_y = speed_b(t)
            out = (1.0 - speed_x - speed_y) * d + speed_y * y_next
            if x_ref is not None:
                out = out + speed_x * x_ref[tile(t), :]
            out_ref[tile(t), :] = out + 0.25 * total
        carried = turned
        d, n, d_turned, n_turned = d_next, n_next, d_turned_next, n_turned_next


def kernel(
    value, density, n, dn,
    v, d, hv, hd, mass, crowd, passing,
    load_sem, edge_send, edge_recv, mass_send, mass_recv, x_send, x_recv, pass_send, pass_recv,
):
    vel, pos = lax.axis_index("vel"), lax.axis_index("pos")
    above, below = lax.rem(pos + 1, POS), lax.rem(pos + POS - 1, POS)
    low = vel < VEL // 2
    value_to = jnp.where(low, above, below)
    density_to = jnp.where(low, below, above)
    near = jnp.where(low, 0, 1)
    far = 1 - near
    has_lower, has_upper = vel > 0, vel < VEL - 1
    half = POS // 2
    place_x = lax.rem(pos, half)
    bottom, top = place_x == 0, place_x == half - 1
    at_end = jnp.logical_or(bottom, top)
    twin = lax.rem(pos + half, POS)
    other_end = jnp.where(bottom, pos + half - 1, pos - half + 1)
    high = jnp.logical_not(low)
    value_long = jnp.logical_or(jnp.logical_and(top, low), jnp.logical_and(bottom, high))
    density_long = jnp.logical_and(at_end, jnp.logical_not(value_long))

    barrier = pltpu.get_barrier_semaphore()
    for other in (above, below):
        pl.semaphore_signal(barrier, inc=1, device_id={"pos": other}, device_id_type=MESH)
    for k in range(1, VEL):
        pl.semaphore_signal(barrier, inc=1, device_id={"vel": lax.rem(vel + k, VEL)}, device_id_type=MESH)

    @pl.when(at_end)
    def _():
        pl.semaphore_signal(barrier, inc=1, device_id={"pos": twin}, device_id_type=MESH)
        pl.semaphore_signal(barrier, inc=1, device_id={"pos": other_end}, device_id_type=MESH)

    load_d = pltpu.make_async_copy(density, d.at[:, pl.ds(1, ROWS)], load_sem.at[0])
    load_v = pltpu.make_async_copy(value, v.at[:, pl.ds(1, ROWS)], load_sem.at[1])
    pl.semaphore_wait(barrier, jnp.where(at_end, 2 + VEL - 1 + 2, 2 + VEL - 1))

    def x_copies(a):
        one = pl.ds(a, 1)
        return (
            pltpu.make_async_remote_copy(
                value.at[far, one], hv.at[one], x_send.at[0, a], x_recv.at[0, a],
                device_id={"pos": value_to}, device_id_type=MESH),
            pltpu.make_async_remote_copy(
                density.at[near, one], hd.at[one], x_send.at[1, a], x_recv.at[1, a],
                device_id={"pos": density_to}, device_id_type=MESH),
        )

    def x_halves(half):
        part = pl.ds(half * (GRID_V // 2), GRID_V // 2)
        return [
            pltpu.make_async_remote_copy(
                source.at[row, LAST, part], target.at[LAST, part], x_send.at[kind, LAST + 2 * half],
                x_recv.at[kind, LAST + 2 * half], device_id={"pos": to}, device_id_type=MESH)
            for kind, (source, row, target, to) in enumerate(
                ((value, far, hv, value_to), (density, near, hd, density_to)))
        ]

    def start_x(a):
        for copy in x_halves(0) + x_halves(1) if a == LAST else x_copies(a):
            copy.start()

    def start_x_passed(a):
        one, k = pl.ds(a, 1), a - PASSED[0]
        for kind, (copy, source, row, crosses) in enumerate(
            zip(x_copies(a), (value, density), (far, near), (value_long, density_long))
        ):
            first_leg = pltpu.make_async_remote_copy(
                source.at[row, one], passing.at[pl.ds(k, 1)], x_send.at[kind, a], pass_recv.at[k],
                device_id={"pos": other_end}, device_id_type=MESH)
            pl.when(crosses)(first_leg.start)
            pl.when(jnp.logical_not(crosses))(copy.start)

    def second_leg(kind, a):
        k = a - PASSED[0]
        return pltpu.make_async_remote_copy(
            passing.at[pl.ds(k, 1)], (hv, hd)[kind].at[pl.ds(a, 1)], pass_send.at[k], x_recv.at[kind, a],
            device_id={"pos": twin}, device_id_type=MESH)

    def pass_on(a):
        @pl.when(at_end)
        def _():
            k = a - PASSED[0]
            first_leg = pltpu.make_async_remote_copy(
                value.at[far, pl.ds(a, 1)], passing.at[pl.ds(k, 1)], x_send.at[0, a], pass_recv.at[k],
                device_id={"pos": other_end}, device_id_type=MESH)
            first_leg.wait_recv()
            pl.when(density_long)(lambda: second_leg(0, a).start())
            pl.when(value_long)(lambda: second_leg(1, a).start())

    def edge_copies(k, source, target):
        to_upper = pltpu.make_async_remote_copy(
            source.at[:, pl.ds(ROWS - 1, 1)], target.at[:, pl.ds(0, 1)], edge_send.at[k, 0], edge_recv.at[k, 0],
            device_id={"vel": lax.rem(vel + 1, VEL)}, device_id_type=MESH)
        to_lower = pltpu.make_async_remote_copy(
            source.at[:, pl.ds(0, 1)], target.at[:, pl.ds(ROWS + 1, 1)], edge_send.at[k, 1], edge_recv.at[k, 1],
            device_id={"vel": lax.rem(vel + VEL - 1, VEL)}, device_id_type=MESH)
        return to_upper, to_lower

    def start_pair(pair):
        to_upper, to_lower = pair

        @pl.when(has_upper)
        def _():
            to_upper.start()

        @pl.when(has_lower)
        def _():
            to_lower.start()

    def receive_pair(pair):
        to_upper, to_lower = pair

        @pl.when(has_lower)
        def _():
            to_upper.wait_recv()

        @pl.when(has_upper)
        def _():
            to_lower.wait_recv()

    def sent_pair(pair):
        to_upper, to_lower = pair

        @pl.when(has_upper)
        def _():
            to_upper.wait_send()

        @pl.when(has_lower)
        def _():
            to_lower.wait_send()

    edges_v, edges_d = edge_copies(0, value, v), edge_copies(1, density, d)
    for a in ORDER:
        (start_x_passed if a in PASSED else start_x)(a)
        if a == ORDER[0]:
            start_pair(edges_v)
            load_d.start()
            load_v.start()
        if a == ORDER[1]:
            start_pair(edges_d)

    load_d.wait()
    place = sublane()

    def add_row(i, sums):
        parts = []
        for r in range(2):
            total = sums[r]
            for t in range(TILES):
                total = total + d[r, i + 1, tile(t), :]
            parts.append(total)
        return tuple(parts)

    zero = jnp.zeros((TILE, NY), F32)
    sums = lax.fori_loop(0, ROWS, add_row, (zero, zero))
    sums = [jnp.sum(s, axis=0, keepdims=True) for s in sums]
    mass[vel] = jnp.where(place == 0, sums[0], sums[1])
    mass_copies = [
        pltpu.make_async_remote_copy(
            mass.at[vel], mass.at[vel], mass_send.at[k], mass_recv.at[k],
            device_id={"vel": lax.rem(vel + k, VEL)}, device_id_type=MESH)
        for k in range(1, VEL)
    ]
    for copy in mass_copies:
        copy.start()
    load_v.wait()

    def repeat_edges(field, rows):
        @pl.when(jnp.logical_not(has_lower))
        def _():
            for r in rows:
                field[r, 0] = field[r, 1]

        @pl.when(jnp.logical_not(has_upper))
        def _():
            for r in rows:
                field[r, ROWS + 1] = field[r, ROWS]

    repeat_edges(v, (0, 1))
    repeat_edges(d, (0, 1))
    for copy in mass_copies:
        copy.wait_recv()
    total = (mass[0] + mass[1]) + (mass[2] + mass[3])
    total = total / (GRID_V * GRID_V)
    total = CROWDING * total * total
    crowd[0] = jnp.broadcast_to(total[0:1], (TILE, NY))
    crowd[1] = jnp.broadcast_to(total[1:2], (TILE, NY))

    def speed_a(a):
        index = (vel * ROWS + a).astype(F32)
        return jnp.abs(COURANT * ((index + 0.5 - GRID_V / 2) / (GRID_V / 2)))

    def value_row(row, a, x_ref, **tiles):
        value_slab(v.at[row, a + 1], v.at[row, a + 2], v.at[row, a], x_ref, crowd[row], speed_a(a), n.at[row, a + 1], **tiles)

    def density_row(row, a, x_ref, out_ref, **tiles):
        density_slab(
            n.at[row, a + 1], n.at[row, a + 2], n.at[row, a],
            d.at[row, a + 1], d.at[row, a + 2], d.at[row, a], x_ref, speed_a(a), out_ref, **tiles)

    def arrive(a):
        for copy in x_copies(a):
            copy.wait_recv()

    def finish_far(a, first=0, stop=TILES):
        speed_x = speed_a(a)
        for t in range(first, stop):
            dn[far, a, tile(t), :] = dn[far, a, tile(t), :] + speed_x * hd[a, tile(t), :]

    def near_density(a, **tiles):
        density_row(near, a, d.at[far, a + 1], dn.at[near, a], **tiles)

    @pl.loop(1, ROWS - 1)
    def _(a):
        value_row(far, a, v.at[near, a + 1])

    @pl.loop(2, ROWS - 2)
    def _(a):
        density_row(far, a, None, dn.at[far, a])

    receive_pair(edges_v)

    @pl.loop(0, 2)
    def _(i):
        a = i * (ROWS - 1)
        arrive(a)
        value_row(far, a, v.at[near, a + 1])
        value_row(near, a, hv.at[a])

    edges_n = edge_copies(2, n.at[:, pl.ds(1, ROWS)], n)
    start_pair(edges_n)
    repeat_edges(n, (0, 1))
    pass_on(1)
    pass_on(2)
    pass_on(3)
    pass_on(4)
    pass_on(5)
    pass_on(6)

    @pl.loop(0, 2)
    def _(i):
        a = 1 + i * (ROWS - 3)
        density_row(far, a, None, dn.at[far, a])

    receive_pair(edges_d)


    def near_step(a):
        arrive(a)
        value_row(near, a, hv.at[a])
        finish_far(a)

    @pl.loop(1, ROWS // 2)
    def _(a):
        near_step(a)

        @pl.when(a > 1)
        def _():
            near_density(a - 1)

    receive_pair(edges_n)

    @pl.loop(0, 2)
    def _(i):
        a = i * (ROWS - 1)
        density_row(far, a, None, dn.at[far, a])
        finish_far(a)

    near_density(0)

    @pl.loop(ROWS // 2, LAST)
    def _(a):
        near_step(a)
        near_density(a - 1)

    middle = TILES // 2
    for half, (first, stop, inner_first, inner_stop) in enumerate(
        ((0, middle, 0, middle - 1), (middle, TILES, middle - 1, TILES))
    ):
        for copy in x_halves(half):
            copy.wait_recv()
        value_row(near, LAST, hv.at[LAST], first=first, stop=stop)
        finish_far(LAST, first, stop)
        near_density(LAST - 1, first=first, stop=stop)
        near_density(LAST, first=inner_first, stop=inner_stop)
        near_density(LAST + 1, first=first, stop=stop)

    for pair in (edges_v, edges_d, edges_n):
        sent_pair(pair)
    for copy in mass_copies:
        copy.wait_send()

    @pl.loop(0, LAST)
    def _(a):
        for copy in x_copies(a):
            copy.wait_send()

    for copy in x_copies(ROWS - 1) + tuple(x_halves(0) + x_halves(1)):
        copy.wait_send()

    @pl.when(at_end)
    def _():
        for a in PASSED:
            second_leg(0, a).wait_send()


def store(n, dn, value_out, density_out, sem):
    copies = []
    for k, (source, target) in enumerate(((n.at[:, pl.ds(1, ROWS)], value_out), (dn, density_out))):
        for r in range(2):
            copies.append(pltpu.make_async_copy(source.at[r], target.at[r], sem.at[2 * k + r]))
    for copy in copies:
        copy.start()
    for copy in copies:
        copy.wait()


def body(value_next, density):
    shape = (2, ROWS, GRID_V, NY)
    haloed = pltpu.VMEM((2, ROWS + 2, GRID_V, NY), F32)
    slab = pltpu.VMEM((ROWS, GRID_V, NY), F32)
    dma = pltpu.SemaphoreType.DMA
    n, dn = pl.pallas_call(
        kernel,
        out_shape=[pltpu.VMEM((2, ROWS + 2, GRID_V, NY), F32), pltpu.VMEM(shape, F32)],
        in_specs=[pl.BlockSpec(memory_space=pltpu.HBM)] * 2,
        out_specs=[pl.BlockSpec(memory_space=pltpu.VMEM)] * 2,
        scratch_shapes=[
            haloed, haloed, slab, slab,
            pltpu.VMEM((VEL, TILE, NY), F32), pltpu.VMEM((2, TILE, NY), F32),
            pltpu.VMEM((len(PASSED), GRID_V, NY), F32),
            dma((2,)), dma((3, 2)), dma((3, 2)), dma((VEL,)), dma((VEL,)),
            dma((2, ROWS + 1)), dma((2, ROWS + 1)), dma((len(PASSED),)), dma((len(PASSED),)),
        ],
        compiler_params=pltpu.CompilerParams(
            collective_id=0, has_side_effects=True, vmem_limit_bytes=52 << 20
        ),
    )(value_next, density)
    return pl.pallas_call(
        store,
        out_shape=[jax.ShapeDtypeStruct(shape, F32)] * 2,
        in_specs=[pl.BlockSpec(memory_space=pltpu.VMEM)] * 2,
        out_specs=[pl.BlockSpec(memory_space=pl.ANY)] * 2,
        scratch_shapes=[dma((4,))],
        compiler_params=pltpu.CompilerParams(vmem_limit_bytes=32 << 20),
    )(n, dn)


def solution(mesh):
    spec = P("pos", "vel", None, None)
    return jax.shard_map(body, mesh=mesh, in_specs=(spec, spec), out_specs=(spec, spec), check_vma=False)
```

```python
import functools

import jax
import jax.numpy as jnp
from jax import lax
from jax.experimental import pallas as pl
from jax.experimental.pallas import tpu as pltpu
from jax.sharding import PartitionSpec as P

MESH = pl.DeviceIdType.MESH
COURANT = 0.4
CROWDING = 0.3
ROWS = 16
GRID_V = 64
NY = 512
TILE = 8
TILES = GRID_V // TILE
VEL = 4
POS = 32
F32 = jnp.float32
ALONG_Y = (1, 2, 3, 4, 5, 6)
ALONG_Z = (7,)

LAST = ROWS - 2
ORDER = (7, 1, 2, 3, 0, ROWS - 1, 4, 5, 6, *range(8, ROWS - 1))
LATE_ORDER = (0, ROWS - 1, 1, 2, 3, 4, 5, 6, *range(8, ROWS - 1))

FIRST = 10


def tile(t):
    return pl.ds(t * TILE, TILE)


def sublane():
    return lax.broadcasted_iota(jnp.int32, (TILE, NY), 0)


def speed_b(t):
    index = (sublane() + t * TILE).astype(F32)
    return jnp.abs(COURANT * ((index + 0.5 - GRID_V / 2) / (GRID_V / 2)))


def value_slab(c_ref, up_ref, dn_ref, x_ref, crowd, speed_x, out_ref, first=0, stop=TILES):
    place = sublane()

    def ahead(t):
        c = c_ref[tile(t), :]
        return c, pltpu.roll(c, TILE - 1, 0)

    begin = max(first - 1, 0)
    c, turned = ahead(begin)
    carried = jnp.zeros((TILE, NY), F32)
    for t in range(begin, stop):
        c_next, turned_next = ahead(t + 1) if t + 1 < TILES else (None, c)
        upper = jnp.where(place == TILE - 1, turned_next, turned) - c
        loss = pltpu.roll(upper * (1.2 + jnp.maximum(upper, 0.0)), 1, 0)
        if t >= first:
            gain = upper * (1.2 - jnp.minimum(upper, 0.0)) - jnp.where(place == 0, carried, loss)
            a_upper = up_ref[tile(t), :] - c
            a_lower = c - dn_ref[tile(t), :]
            gain = gain + a_upper * (1.2 - jnp.minimum(a_upper, 0.0))
            gain = gain - a_lower * (1.2 + jnp.maximum(a_lower, 0.0))
            y_next = pltpu.roll(c, 1 if t < TILES // 2 else NY - 1, 1)
            speed_y = speed_b(t)
            out = (1.0 - speed_x - speed_y) * c + speed_x * x_ref[tile(t), :] + speed_y * y_next
            out_ref[tile(t), :] = out + (0.125 * gain + crowd)
        carried = loss
        c, turned = c_next, turned_next


def density_slab(n_ref, n_up_ref, n_dn_ref, d_ref, d_up_ref, d_dn_ref, x_ref, speed_x, out_ref, first=0, stop=TILES):
    place = sublane()

    def ahead(t):
        d, n = d_ref[tile(t), :], n_ref[tile(t), :]
        return d, n, pltpu.roll(d, TILE - 1, 0), pltpu.roll(n, TILE - 1, 0)

    begin = max(first - 1, 0)
    d, n, d_turned, n_turned = ahead(begin)
    carried = jnp.zeros((TILE, NY), F32)
    for t in range(begin, stop):
        d_next, n_next, d_turned_next, n_turned_next = ahead(t + 1) if t + 1 < TILES else (None, None, d, n)
        last = place == TILE - 1
        d_beyond = jnp.where(last, d_turned_next, d_turned)
        step = n - jnp.where(last, n_turned_next, n_turned)
        flux = (jnp.maximum(step, 0.0) + 0.6) * (d - d_beyond) + step * d_beyond
        turned = pltpu.roll(flux, 1, 0)
        if t >= first:
            total = jnp.where(place == 0, carried, turned) - flux
            d_up, d_dn = d_up_ref[tile(t), :], d_dn_ref[tile(t), :]
            step = n - n_up_ref[tile(t), :]
            total = total - ((jnp.maximum(step, 0.0) + 0.6) * (d - d_up) + step * d_up)
            step = n_dn_ref[tile(t), :] - n
            total = total + ((jnp.maximum(step, 0.0) + 0.6) * (d_dn - d) + step * d)
            y_next = pltpu.roll(d, NY - 1 if t < TILES // 2 else 1, 1)
            speed_y = speed_b(t)
            out = (1.0 - speed_x - speed_y) * d + speed_y * y_next
            if x_ref is not None:
                out = out + speed_x * x_ref[tile(t), :]
            out_ref[tile(t), :] = out + 0.25 * total
        carried = turned
        d, n, d_turned, n_turned = d_next, n_next, d_turned_next, n_turned_next


def kernel(
    value, density, n, dn,
    v, d, hv, hd, mass, crowd, passing,
    load_sem, edge_send, edge_recv, mass_send, mass_recv, x_send, x_recv, pass_send, pass_recv, ready,
):
    vel, pos = lax.axis_index("vel"), lax.axis_index("pos")
    above, below = lax.rem(pos + 1, POS), lax.rem(pos + POS - 1, POS)
    low = vel < VEL // 2
    value_to = jnp.where(low, above, below)
    density_to = jnp.where(low, below, above)
    near = jnp.where(low, 0, 1)
    far = 1 - near
    has_lower, has_upper = vel > 0, vel < VEL - 1
    half = POS // 2
    place_x = lax.rem(pos, half)
    bottom, top = place_x == 0, place_x == half - 1
    at_end = jnp.logical_or(bottom, top)
    lower_top, upper_top = pos == half - 1, pos == POS - 1
    twin = lax.rem(pos + half, POS)
    other_end = jnp.where(bottom, pos + half - 1, pos - half + 1)
    high = jnp.logical_not(low)
    value_long = jnp.logical_or(jnp.logical_and(top, low), jnp.logical_and(bottom, high))
    density_long = jnp.logical_and(at_end, jnp.logical_not(value_long))
    z_steps = (12,)
    via_z = [jnp.where(bottom, pos + step, pos - step) for step in z_steps]
    up_helper = [place_x == half - 1 - step for step in z_steps]
    down_helper = [place_x == step for step in z_steps]
    helper = [jnp.logical_or(u, w) for u, w in zip(up_helper, down_helper)]
    helped = [jnp.where(u, pos + step, pos - step) for u, step in zip(up_helper, z_steps)]
    helped_to = [lax.rem(jnp.where(u, at + 1, at + POS - 1), POS) for u, at in zip(up_helper, helped)]
    any_up, any_down = up_helper[0], down_helper[0]
    helps_value = jnp.logical_or(jnp.logical_and(any_up, low), jnp.logical_and(any_down, high))

    barrier = pltpu.get_barrier_semaphore()

    def announce(**device):
        pl.semaphore_signal(barrier, inc=1, device_id=device, device_id_type=MESH)

    announce(pos=below)
    pl.when(jnp.logical_not(top))(lambda: announce(pos=above))
    for k in range(1, VEL):
        announce(vel=lax.rem(vel + k, VEL))

    @pl.when(bottom)
    def _():
        announce(pos=twin)
        announce(pos=other_end)
        for step in z_steps:
            announce(pos=lax.rem(pos + POS - 1 - step, POS))

    pl.when(lower_top)(lambda: announce(pos=twin))
    for k in range(len(z_steps)):
        pl.when(helper[k])(lambda: announce(pos=helped[k]))
        pl.when(down_helper[k])(lambda: announce(pos=helped_to[k]))

    load_d = pltpu.make_async_copy(density, d.at[:, pl.ds(1, ROWS)], load_sem.at[0])
    load_v = pltpu.make_async_copy(value, v.at[:, pl.ds(1, ROWS)], load_sem.at[1])
    expected = jnp.where(bottom, 6, jnp.where(upper_top, 9, jnp.where(top, 8, jnp.where(any_up, 6, 5))))
    pl.semaphore_wait(barrier, expected)

    def is_ready(**device):
        pl.semaphore_signal(ready, inc=1, device_id=device, device_id_type=MESH)

    @pl.when(top)
    def _():
        is_ready(pos=above)
        is_ready(pos=other_end)
        for step in z_steps:
            is_ready(pos=lax.rem(pos + 1 + step, POS))

    pl.when(upper_top)(lambda: is_ready(pos=twin))

    def x_copies(a):
        one = pl.ds(a, 1)
        return (
            pltpu.make_async_remote_copy(
                value.at[far, one], hv.at[one], x_send.at[0, a], x_recv.at[0, a],
                device_id={"pos": value_to}, device_id_type=MESH),
            pltpu.make_async_remote_copy(
                density.at[near, one], hd.at[one], x_send.at[1, a], x_recv.at[1, a],
                device_id={"pos": density_to}, device_id_type=MESH),
        )

    def x_halves(half):
        part = pl.ds(half * (GRID_V // 2), GRID_V // 2)
        return [
            pltpu.make_async_remote_copy(
                source.at[row, LAST, part], target.at[LAST, part], x_send.at[kind, LAST + 2 * half],
                x_recv.at[kind, LAST + 2 * half], device_id={"pos": to}, device_id_type=MESH)
            for kind, (source, row, target, to) in enumerate(
                ((value, far, hv, value_to), (density, near, hd, density_to)))
        ]

    def copies_of(a):
        return x_halves(0) + x_halves(1) if a == LAST else x_copies(a)

    def first_leg(kind, a, to):
        source = (value.at[far], density.at[near])[kind]
        return pltpu.make_async_remote_copy(
            source.at[pl.ds(a, 1)], passing.at[pl.ds(a - 1, 1)], x_send.at[kind, a], pass_recv.at[a - 1],
            device_id={"pos": to}, device_id_type=MESH)

    def second_leg(kind, a, to):
        return pltpu.make_async_remote_copy(
            passing.at[pl.ds(a - 1, 1)], (hv, hd)[kind].at[pl.ds(a, 1)], pass_send.at[a - 1], x_recv.at[kind, a],
            device_id={"pos": to}, device_id_type=MESH)

    def start_crossing(kind, a):
        if a in ALONG_Y:
            first_leg(kind, a, other_end).start()
        else:
            for copy in copies_of(a)[kind::2]:
                copy.start()

    def start_x(rows):
        @pl.when(jnp.logical_not(at_end))
        def _():
            for a in rows:
                for copy in copies_of(a):
                    copy.start()

        for kind, crosses in enumerate((value_long, density_long)):
            @pl.when(jnp.logical_and(at_end, jnp.logical_not(crosses)))
            def _():
                for a in rows:
                    for copy in copies_of(a)[kind::2]:
                        copy.start()

            @pl.when(crosses)
            def _():
                for a in rows:
                    if a in ALONG_Z:
                        first_leg(kind, a, via_z[0]).start()

            @pl.when(jnp.logical_and(crosses, top))
            def _():
                for a in rows:
                    if a not in ALONG_Z:
                        start_crossing(kind, a)

    def start_x_late():
        for kind, crosses in enumerate((value_long, density_long)):
            @pl.when(jnp.logical_and(crosses, bottom))
            def _():
                for a in LATE_ORDER:
                    start_crossing(kind, a)

    def pass_on(a):
        @pl.when(at_end)
        def _():
            first_leg(0, a, other_end).wait_recv()
            pl.when(density_long)(lambda: second_leg(0, a, twin).start())
            pl.when(value_long)(lambda: second_leg(1, a, twin).start())

    def help_on(a):
        @pl.when(helper[0])
        def _():
            first_leg(0, a, helped[0]).wait_recv()
            pl.when(helps_value)(lambda: second_leg(0, a, helped_to[0]).start())
            pl.when(jnp.logical_not(helps_value))(lambda: second_leg(1, a, helped_to[0]).start())

    def edge_copies(k, source, target):
        to_upper = pltpu.make_async_remote_copy(
            source.at[:, pl.ds(ROWS - 1, 1)], target.at[:, pl.ds(0, 1)], edge_send.at[k, 0], edge_recv.at[k, 0],
            device_id={"vel": lax.rem(vel + 1, VEL)}, device_id_type=MESH)
        to_lower = pltpu.make_async_remote_copy(
            source.at[:, pl.ds(0, 1)], target.at[:, pl.ds(ROWS + 1, 1)], edge_send.at[k, 1], edge_recv.at[k, 1],
            device_id={"vel": lax.rem(vel + VEL - 1, VEL)}, device_id_type=MESH)
        return to_upper, to_lower

    def start_pair(pair):
        to_upper, to_lower = pair

        @pl.when(has_upper)
        def _():
            to_upper.start()

        @pl.when(has_lower)
        def _():
            to_lower.start()

    def receive_pair(pair):
        to_upper, to_lower = pair

        @pl.when(has_lower)
        def _():
            to_upper.wait_recv()

        @pl.when(has_upper)
        def _():
            to_lower.wait_recv()

    def sent_pair(pair):
        to_upper, to_lower = pair

        @pl.when(has_upper)
        def _():
            to_upper.wait_send()

        @pl.when(has_lower)
        def _():
            to_lower.wait_send()

    edges_v, edges_d = edge_copies(0, value, v), edge_copies(1, density, d)
    start_x(ORDER[:1])
    start_pair(edges_v)
    load_d.start()
    load_v.start()
    start_x(ORDER[1:3])
    start_pair(edges_d)
    start_x(ORDER[3:FIRST])

    load_d.wait()
    place = sublane()

    def add_row(i, sums):
        parts = []
        for r in range(2):
            total = sums[r]
            for t in range(TILES):
                total = total + d[r, i + 1, tile(t), :]
            parts.append(total)
        return tuple(parts)

    zero = jnp.zeros((TILE, NY), F32)
    sums = lax.fori_loop(0, ROWS, add_row, (zero, zero))
    sums = [jnp.sum(s, axis=0, keepdims=True) for s in sums]
    mass[vel] = jnp.where(place == 0, sums[0], sums[1])
    mass_copies = [
        pltpu.make_async_remote_copy(
            mass.at[vel], mass.at[vel], mass_send.at[k], mass_recv.at[k],
            device_id={"vel": lax.rem(vel + k, VEL)}, device_id_type=MESH)
        for k in range(1, VEL)
    ]
    for copy in mass_copies:
        copy.start()
    pl.when(bottom)(lambda: pl.semaphore_wait(ready, 2))
    start_x_late()
    load_v.wait()

    def repeat_edges(field, rows):
        @pl.when(jnp.logical_not(has_lower))
        def _():
            for r in rows:
                field[r, 0] = field[r, 1]

        @pl.when(jnp.logical_not(has_upper))
        def _():
            for r in rows:
                field[r, ROWS + 1] = field[r, ROWS]

    repeat_edges(v, (0, 1))
    repeat_edges(d, (0, 1))
    for copy in mass_copies:
        copy.wait_recv()
    total = (mass[0] + mass[1]) + (mass[2] + mass[3])
    total = total / (GRID_V * GRID_V)
    total = CROWDING * total * total
    crowd[0] = jnp.broadcast_to(total[0:1], (TILE, NY))
    crowd[1] = jnp.broadcast_to(total[1:2], (TILE, NY))

    def speed_a(a):
        index = (vel * ROWS + a).astype(F32)
        return jnp.abs(COURANT * ((index + 0.5 - GRID_V / 2) / (GRID_V / 2)))

    def value_row(row, a, x_ref, **tiles):
        value_slab(v.at[row, a + 1], v.at[row, a + 2], v.at[row, a], x_ref, crowd[row], speed_a(a), n.at[row, a + 1], **tiles)

    def density_row(row, a, x_ref, out_ref, **tiles):
        density_slab(
            n.at[row, a + 1], n.at[row, a + 2], n.at[row, a],
            d.at[row, a + 1], d.at[row, a + 2], d.at[row, a], x_ref, speed_a(a), out_ref, **tiles)

    def arrive(a):
        for copy in x_copies(a):
            copy.wait_recv()

    def finish_far(a, first=0, stop=TILES):
        speed_x = speed_a(a)
        for t in range(first, stop):
            dn[far, a, tile(t), :] = dn[far, a, tile(t), :] + speed_x * hd[a, tile(t), :]

    def near_density(a, **tiles):
        density_row(near, a, d.at[far, a + 1], dn.at[near, a], **tiles)

    @pl.loop(1, ROWS - 1)
    def _(a):
        value_row(far, a, v.at[near, a + 1])

    pl.when(jnp.logical_or(lower_top, any_down))(lambda: pl.semaphore_wait(ready, 1))
    for a in ALONG_Z:
        help_on(a)
    start_x(ORDER[FIRST:])

    @pl.loop(2, ROWS - 2)
    def _(a):
        density_row(far, a, None, dn.at[far, a])

    receive_pair(edges_v)

    @pl.loop(0, 2)
    def _(i):
        a = i * (ROWS - 1)
        arrive(a)
        value_row(far, a, v.at[near, a + 1])
        value_row(near, a, hv.at[a])

    edges_n = edge_copies(2, n.at[:, pl.ds(1, ROWS)], n)
    start_pair(edges_n)
    repeat_edges(n, (0, 1))
    pass_on(1)
    pass_on(2)
    pass_on(3)

    @pl.loop(0, 2)
    def _(i):
        a = 1 + i * (ROWS - 3)
        density_row(far, a, None, dn.at[far, a])

    receive_pair(edges_d)


    def near_step(a):
        arrive(a)
        value_row(near, a, hv.at[a])
        finish_far(a)

    @pl.loop(1, ROWS // 2)
    def _(a):
        pl.when(a + 3 <= ALONG_Y[-1])(lambda: pass_on(a + 3))
        near_step(a)

        @pl.when(a > 1)
        def _():
            near_density(a - 1)

    receive_pair(edges_n)

    @pl.loop(0, 2)
    def _(i):
        a = i * (ROWS - 1)
        density_row(far, a, None, dn.at[far, a])
        finish_far(a)

    near_density(0)

    @pl.loop(ROWS // 2, LAST)
    def _(a):
        near_step(a)
        near_density(a - 1)

    middle = TILES // 2
    for half, (first, stop, inner_first, inner_stop) in enumerate(
        ((0, middle, 0, middle - 1), (middle, TILES, middle - 1, TILES))
    ):
        for copy in x_halves(half):
            copy.wait_recv()
        value_row(near, LAST, hv.at[LAST], first=first, stop=stop)
        finish_far(LAST, first, stop)
        near_density(LAST - 1, first=first, stop=stop)
        near_density(LAST, first=inner_first, stop=inner_stop)
        near_density(LAST + 1, first=first, stop=stop)

    for pair in (edges_v, edges_d, edges_n):
        sent_pair(pair)
    for copy in mass_copies:
        copy.wait_send()

    @pl.loop(0, LAST)
    def _(a):
        for copy in x_copies(a):
            copy.wait_send()

    for copy in x_copies(ROWS - 1) + tuple(x_halves(0) + x_halves(1)):
        copy.wait_send()

    @pl.when(at_end)
    def _():
        for a in ALONG_Y:
            second_leg(0, a, twin).wait_send()

    for a in ALONG_Z:
        pl.when(helper[0])(lambda: second_leg(0, a, helped_to[0]).wait_send())


def store(n, dn, value_out, density_out, sem):
    copies = []
    for k, (source, target) in enumerate(((n.at[:, pl.ds(1, ROWS)], value_out), (dn, density_out))):
        for r in range(2):
            copies.append(pltpu.make_async_copy(source.at[r], target.at[r], sem.at[2 * k + r]))
    for copy in copies:
        copy.start()
    for copy in copies:
        copy.wait()


def body(value_next, density):
    shape = (2, ROWS, GRID_V, NY)
    haloed = pltpu.VMEM((2, ROWS + 2, GRID_V, NY), F32)
    slab = pltpu.VMEM((ROWS, GRID_V, NY), F32)
    dma = pltpu.SemaphoreType.DMA
    n, dn = pl.pallas_call(
        kernel,
        out_shape=[pltpu.VMEM((2, ROWS + 2, GRID_V, NY), F32), pltpu.VMEM(shape, F32)],
        in_specs=[pl.BlockSpec(memory_space=pltpu.HBM)] * 2,
        out_specs=[pl.BlockSpec(memory_space=pltpu.VMEM)] * 2,
        scratch_shapes=[
            haloed, haloed, slab, slab,
            pltpu.VMEM((VEL, TILE, NY), F32), pltpu.VMEM((2, TILE, NY), F32),
            pltpu.VMEM((len(ALONG_Y + ALONG_Z), GRID_V, NY), F32),
            dma((2,)), dma((3, 2)), dma((3, 2)), dma((VEL,)), dma((VEL,)),
            dma((2, ROWS + 1)), dma((2, ROWS + 1)), dma((len(ALONG_Y + ALONG_Z),)), dma((len(ALONG_Y + ALONG_Z),)), pltpu.SemaphoreType.REGULAR,
        ],
        compiler_params=pltpu.CompilerParams(
            collective_id=0, has_side_effects=True, vmem_limit_bytes=52 << 20
        ),
    )(value_next, density)
    return pl.pallas_call(
        store,
        out_shape=[jax.ShapeDtypeStruct(shape, F32)] * 2,
        in_specs=[pl.BlockSpec(memory_space=pltpu.VMEM)] * 2,
        out_specs=[pl.BlockSpec(memory_space=pl.ANY)] * 2,
        scratch_shapes=[dma((4,))],
        compiler_params=pltpu.CompilerParams(vmem_limit_bytes=32 << 20),
    )(n, dn)


def solution(mesh):
    spec = P("pos", "vel", None, None)
    return jax.shard_map(body, mesh=mesh, in_specs=(spec, spec), out_specs=(spec, spec), check_vma=False)
```

```python
import functools

import jax
import jax.numpy as jnp
from jax import lax
from jax.experimental import pallas as pl
from jax.experimental.pallas import tpu as pltpu
from jax.sharding import PartitionSpec as P

MESH = pl.DeviceIdType.MESH
COURANT = 0.4
CROWDING = 0.3
ROWS = 16
GRID_V = 64
NY = 512
TILE = 8
TILES = GRID_V // TILE
VEL = 4
POS = 32
F32 = jnp.float32
ALONG_Y = (1, 2, 3, 4)
DOWN_Y = (1, 2, 3, 4, 5)
ALONG_Z = (7, 8)
NEXT_Z = (7,)

LAST = ROWS - 2
ORDER = (7, 8, 0, ROWS - 1, 1, 2, 3, 4, 5, 6, *range(9, ROWS - 1))
LATE_ORDER = (0, ROWS - 1, 1, 2, 3, 4, 5, 6, *range(9, ROWS - 1))

FIRST = 10


def tile(t):
    return pl.ds(t * TILE, TILE)


def sublane():
    return lax.broadcasted_iota(jnp.int32, (TILE, NY), 0)


def speed_b(t):
    index = (sublane() + t * TILE).astype(F32)
    return jnp.abs(COURANT * ((index + 0.5 - GRID_V / 2) / (GRID_V / 2)))


def value_slab(c_ref, up_ref, dn_ref, x_ref, crowd, speed_x, out_ref, first=0, stop=TILES):
    place = sublane()

    def ahead(t):
        c = c_ref[tile(t), :]
        return c, pltpu.roll(c, TILE - 1, 0)

    begin = max(first - 1, 0)
    c, turned = ahead(begin)
    carried = jnp.zeros((TILE, NY), F32)
    for t in range(begin, stop):
        c_next, turned_next = ahead(t + 1) if t + 1 < TILES else (None, c)
        upper = jnp.where(place == TILE - 1, turned_next, turned) - c
        loss = pltpu.roll(upper * (1.2 + jnp.maximum(upper, 0.0)), 1, 0)
        if t >= first:
            gain = upper * (1.2 - jnp.minimum(upper, 0.0)) - jnp.where(place == 0, carried, loss)
            a_upper = up_ref[tile(t), :] - c
            a_lower = c - dn_ref[tile(t), :]
            gain = gain + a_upper * (1.2 - jnp.minimum(a_upper, 0.0))
            gain = gain - a_lower * (1.2 + jnp.maximum(a_lower, 0.0))
            y_next = pltpu.roll(c, 1 if t < TILES // 2 else NY - 1, 1)
            speed_y = speed_b(t)
            out = (1.0 - speed_x - speed_y) * c + speed_x * x_ref[tile(t), :] + speed_y * y_next
            out_ref[tile(t), :] = out + (0.125 * gain + crowd)
        carried = loss
        c, turned = c_next, turned_next


def density_slab(n_ref, n_up_ref, n_dn_ref, d_ref, d_up_ref, d_dn_ref, x_ref, speed_x, out_ref, first=0, stop=TILES):
    place = sublane()

    def ahead(t):
        d, n = d_ref[tile(t), :], n_ref[tile(t), :]
        return d, n, pltpu.roll(d, TILE - 1, 0), pltpu.roll(n, TILE - 1, 0)

    begin = max(first - 1, 0)
    d, n, d_turned, n_turned = ahead(begin)
    carried = jnp.zeros((TILE, NY), F32)
    for t in range(begin, stop):
        d_next, n_next, d_turned_next, n_turned_next = ahead(t + 1) if t + 1 < TILES else (None, None, d, n)
        last = place == TILE - 1
        d_beyond = jnp.where(last, d_turned_next, d_turned)
        step = n - jnp.where(last, n_turned_next, n_turned)
        flux = (jnp.maximum(step, 0.0) + 0.6) * (d - d_beyond) + step * d_beyond
        turned = pltpu.roll(flux, 1, 0)
        if t >= first:
            total = jnp.where(place == 0, carried, turned) - flux
            d_up, d_dn = d_up_ref[tile(t), :], d_dn_ref[tile(t), :]
            step = n - n_up_ref[tile(t), :]
            total = total - ((jnp.maximum(step, 0.0) + 0.6) * (d - d_up) + step * d_up)
            step = n_dn_ref[tile(t), :] - n
            total = total + ((jnp.maximum(step, 0.0) + 0.6) * (d_dn - d) + step * d)
            y_next = pltpu.roll(d, NY - 1 if t < TILES // 2 else 1, 1)
            speed_y = speed_b(t)
            out = (1.0 - speed_x - speed_y) * d + speed_y * y_next
            if x_ref is not None:
                out = out + speed_x * x_ref[tile(t), :]
            out_ref[tile(t), :] = out + 0.25 * total
        carried = turned
        d, n, d_turned, n_turned = d_next, n_next, d_turned_next, n_turned_next


def kernel(
    value, density, n, dn,
    v, d, hv, hd, mass, crowd, passing,
    load_sem, edge_send, edge_recv, mass_send, mass_recv, x_send, x_recv, pass_send, pass_recv, ready,
):
    vel, pos = lax.axis_index("vel"), lax.axis_index("pos")
    above, below = lax.rem(pos + 1, POS), lax.rem(pos + POS - 1, POS)
    low = vel < VEL // 2
    value_to = jnp.where(low, above, below)
    density_to = jnp.where(low, below, above)
    near = jnp.where(low, 0, 1)
    far = 1 - near
    has_lower, has_upper = vel > 0, vel < VEL - 1
    half = POS // 2
    place_x = lax.rem(pos, half)
    bottom, top = place_x == 0, place_x == half - 1
    at_end = jnp.logical_or(bottom, top)
    lower_top, upper_top = pos == half - 1, pos == POS - 1
    twin = lax.rem(pos + half, POS)
    other_end = jnp.where(bottom, pos + half - 1, pos - half + 1)
    high = jnp.logical_not(low)
    value_long = jnp.logical_or(jnp.logical_and(top, low), jnp.logical_and(bottom, high))
    density_long = jnp.logical_and(at_end, jnp.logical_not(value_long))
    up_1, down_1 = place_x == 3, place_x == 12
    up_2, down_2 = place_x == 7, place_x == 8
    any_1, any_2 = jnp.logical_or(up_1, down_1), jnp.logical_or(up_2, down_2)
    helper = jnp.logical_or(any_1, any_2)
    any_up = jnp.logical_or(up_1, up_2)
    reach = jnp.where(any_2, -4, 12)
    helped = jnp.where(any_up, pos + reach, pos - reach)
    helped_to = lax.rem(jnp.where(any_up, helped + 1, helped + POS - 1), POS)
    helps_value = jnp.logical_and(helper, jnp.where(any_up, low, high))
    via_z = jnp.where(bottom, pos + 12, jnp.where(top, pos - 12, jnp.where(up_1, pos + 4, pos - 4)))
    value_next_z = jnp.logical_and(any_1, helps_value)
    density_next_z = jnp.logical_and(any_1, jnp.logical_not(helps_value))

    barrier = pltpu.get_barrier_semaphore()

    def announce(**device):
        pl.semaphore_signal(barrier, inc=1, device_id=device, device_id_type=MESH)

    announce(pos=below)
    pl.when(jnp.logical_not(top))(lambda: announce(pos=above))
    for k in range(1, VEL):
        announce(vel=lax.rem(vel + k, VEL))

    @pl.when(bottom)
    def _():
        announce(pos=twin)
        announce(pos=other_end)

    pl.when(lower_top)(lambda: announce(pos=twin))
    pl.when(helper)(lambda: announce(pos=helped))
    pl.when(any_1)(lambda: announce(pos=helped_to))
    pl.when(place_x == 4)(lambda: announce(pos=pos + 3))
    pl.when(place_x == 11)(lambda: announce(pos=pos - 3))

    load_d = pltpu.make_async_copy(density, d.at[:, pl.ds(1, ROWS)], load_sem.at[0])
    load_v = pltpu.make_async_copy(value, v.at[:, pl.ds(1, ROWS)], load_sem.at[1])
    expected = jnp.where(bottom, 7, jnp.where(upper_top, 9, jnp.where(top, 8, jnp.where(helper, 6, 5))))
    pl.semaphore_wait(barrier, expected)

    def is_ready(**device):
        pl.semaphore_signal(ready, inc=1, device_id=device, device_id_type=MESH)

    @pl.when(top)
    def _():
        is_ready(pos=above)
        is_ready(pos=other_end)
        is_ready(pos=lax.rem(pos + 13, POS))

    pl.when(upper_top)(lambda: is_ready(pos=twin))
    pl.when(bottom)(lambda: is_ready(pos=lax.rem(pos + POS - 13, POS)))

    def x_copies(a):
        one = pl.ds(a, 1)
        return (
            pltpu.make_async_remote_copy(
                value.at[far, one], hv.at[one], x_send.at[0, a], x_recv.at[0, a],
                device_id={"pos": value_to}, device_id_type=MESH),
            pltpu.make_async_remote_copy(
                density.at[near, one], hd.at[one], x_send.at[1, a], x_recv.at[1, a],
                device_id={"pos": density_to}, device_id_type=MESH),
        )

    def x_halves(half):
        part = pl.ds(half * (GRID_V // 2), GRID_V // 2)
        return [
            pltpu.make_async_remote_copy(
                source.at[row, LAST, part], target.at[LAST, part], x_send.at[kind, LAST + 2 * half],
                x_recv.at[kind, LAST + 2 * half], device_id={"pos": to}, device_id_type=MESH)
            for kind, (source, row, target, to) in enumerate(
                ((value, far, hv, value_to), (density, near, hd, density_to)))
        ]

    def copies_of(a):
        return x_halves(0) + x_halves(1) if a == LAST else x_copies(a)

    def first_leg(kind, a, to):
        source = (value.at[far], density.at[near])[kind]
        return pltpu.make_async_remote_copy(
            source.at[pl.ds(a, 1)], passing.at[pl.ds(a - 1, 1)], x_send.at[kind, a], pass_recv.at[a - 1],
            device_id={"pos": to}, device_id_type=MESH)

    def second_leg(kind, a, to):
        return pltpu.make_async_remote_copy(
            passing.at[pl.ds(a - 1, 1)], (hv, hd)[kind].at[pl.ds(a, 1)], pass_send.at[a - 1], x_recv.at[kind, a],
            device_id={"pos": to}, device_id_type=MESH)

    def start_crossing(kind, a, passed=ALONG_Y):
        if a in passed:
            first_leg(kind, a, other_end).start()
        else:
            for copy in copies_of(a)[kind::2]:
                copy.start()

    special = jnp.logical_or(at_end, any_1)

    def start_x(rows):
        @pl.when(jnp.logical_not(special))
        def _():
            for a in rows:
                for copy in copies_of(a):
                    copy.start()

        for kind, (crosses, turns) in enumerate(((value_long, value_next_z), (density_long, density_next_z))):
            @pl.when(jnp.logical_and(special, jnp.logical_not(jnp.logical_or(crosses, turns))))
            def _():
                for a in rows:
                    for copy in copies_of(a)[kind::2]:
                        copy.start()

            @pl.when(turns)
            def _():
                for a in rows:
                    if a in NEXT_Z:
                        first_leg(kind, a, via_z).start()
                    else:
                        for copy in copies_of(a)[kind::2]:
                            copy.start()

            @pl.when(crosses)
            def _():
                for a in rows:
                    if a in ALONG_Z:
                        first_leg(kind, a, via_z).start()

            @pl.when(jnp.logical_and(crosses, top))
            def _():
                for a in rows:
                    if a not in ALONG_Z:
                        start_crossing(kind, a)

    def start_x_late():
        for kind, crosses in enumerate((value_long, density_long)):
            @pl.when(jnp.logical_and(crosses, bottom))
            def _():
                for a in LATE_ORDER:
                    start_crossing(kind, a, DOWN_Y)

    def pass_on(a, where=at_end):
        @pl.when(where)
        def _():
            first_leg(0, a, other_end).wait_recv()
            pl.when(density_long)(lambda: second_leg(0, a, twin).start())
            pl.when(value_long)(lambda: second_leg(1, a, twin).start())

    def helps_with(a):
        return helper if a in NEXT_Z else any_1

    def help_on(a):
        @pl.when(helps_with(a))
        def _():
            first_leg(0, a, helped).wait_recv()
            pl.when(helps_value)(lambda: second_leg(0, a, helped_to).start())
            pl.when(jnp.logical_not(helps_value))(lambda: second_leg(1, a, helped_to).start())

    def edge_copies(k, source, target):
        to_upper = pltpu.make_async_remote_copy(
            source.at[:, pl.ds(ROWS - 1, 1)], target.at[:, pl.ds(0, 1)], edge_send.at[k, 0], edge_recv.at[k, 0],
            device_id={"vel": lax.rem(vel + 1, VEL)}, device_id_type=MESH)
        to_lower = pltpu.make_async_remote_copy(
            source.at[:, pl.ds(0, 1)], target.at[:, pl.ds(ROWS + 1, 1)], edge_send.at[k, 1], edge_recv.at[k, 1],
            device_id={"vel": lax.rem(vel + VEL - 1, VEL)}, device_id_type=MESH)
        return to_upper, to_lower

    def start_pair(pair):
        to_upper, to_lower = pair

        @pl.when(has_upper)
        def _():
            to_upper.start()

        @pl.when(has_lower)
        def _():
            to_lower.start()

    def receive_pair(pair):
        to_upper, to_lower = pair

        @pl.when(has_lower)
        def _():
            to_upper.wait_recv()

        @pl.when(has_upper)
        def _():
            to_lower.wait_recv()

    def sent_pair(pair):
        to_upper, to_lower = pair

        @pl.when(has_upper)
        def _():
            to_upper.wait_send()

        @pl.when(has_lower)
        def _():
            to_lower.wait_send()

    edges_v, edges_d = edge_copies(0, value, v), edge_copies(1, density, d)
    start_x(ORDER[:1])
    start_pair(edges_v)
    load_d.start()
    load_v.start()
    start_x(ORDER[1:3])
    start_pair(edges_d)
    start_x(ORDER[3:FIRST])

    load_d.wait()
    place = sublane()

    def add_row(i, sums):
        parts = []
        for r in range(2):
            total = sums[r]
            for t in range(TILES):
                total = total + d[r, i + 1, tile(t), :]
            parts.append(total)
        return tuple(parts)

    zero = jnp.zeros((TILE, NY), F32)
    sums = lax.fori_loop(0, ROWS, add_row, (zero, zero))
    sums = [jnp.sum(s, axis=0, keepdims=True) for s in sums]
    mass[vel] = jnp.where(place == 0, sums[0], sums[1])
    mass_copies = [
        pltpu.make_async_remote_copy(
            mass.at[vel], mass.at[vel], mass_send.at[k], mass_recv.at[k],
            device_id={"vel": lax.rem(vel + k, VEL)}, device_id_type=MESH)
        for k in range(1, VEL)
    ]
    for copy in mass_copies:
        copy.start()
    pl.when(bottom)(lambda: pl.semaphore_wait(ready, 2))
    start_x_late()
    load_v.wait()

    def repeat_edges(field, rows):
        @pl.when(jnp.logical_not(has_lower))
        def _():
            for r in rows:
                field[r, 0] = field[r, 1]

        @pl.when(jnp.logical_not(has_upper))
        def _():
            for r in rows:
                field[r, ROWS + 1] = field[r, ROWS]

    repeat_edges(v, (0, 1))
    repeat_edges(d, (0, 1))
    for copy in mass_copies:
        copy.wait_recv()
    total = (mass[0] + mass[1]) + (mass[2] + mass[3])
    total = total / (GRID_V * GRID_V)
    total = CROWDING * total * total
    crowd[0] = jnp.broadcast_to(total[0:1], (TILE, NY))
    crowd[1] = jnp.broadcast_to(total[1:2], (TILE, NY))

    def speed_a(a):
        index = (vel * ROWS + a).astype(F32)
        return jnp.abs(COURANT * ((index + 0.5 - GRID_V / 2) / (GRID_V / 2)))

    def value_row(row, a, x_ref, **tiles):
        value_slab(v.at[row, a + 1], v.at[row, a + 2], v.at[row, a], x_ref, crowd[row], speed_a(a), n.at[row, a + 1], **tiles)

    def density_row(row, a, x_ref, out_ref, **tiles):
        density_slab(
            n.at[row, a + 1], n.at[row, a + 2], n.at[row, a],
            d.at[row, a + 1], d.at[row, a + 2], d.at[row, a], x_ref, speed_a(a), out_ref, **tiles)

    def arrive(a):
        for copy in x_copies(a):
            copy.wait_recv()

    def finish_far(a, first=0, stop=TILES):
        speed_x = speed_a(a)
        for t in range(first, stop):
            dn[far, a, tile(t), :] = dn[far, a, tile(t), :] + speed_x * hd[a, tile(t), :]

    def near_density(a, **tiles):
        density_row(near, a, d.at[far, a + 1], dn.at[near, a], **tiles)

    def inner_values(here):
        @pl.loop(jnp.where(here, 1, ROWS - 1), ROWS - 1)
        def _(a):
            value_row(far, a, v.at[near, a + 1])

    inner_values(at_end)

    receive_pair(edges_v)

    @pl.loop(0, 2)
    def _(i):
        a = i * (ROWS - 1)
        arrive(a)
        value_row(far, a, v.at[near, a + 1])
        value_row(near, a, hv.at[a])

    edges_n = edge_copies(2, n.at[:, pl.ds(1, ROWS)], n)
    start_pair(edges_n)
    repeat_edges(n, (0, 1))
    inner_values(jnp.logical_not(at_end))
    pl.when(jnp.logical_or(lower_top, any_1))(lambda: pl.semaphore_wait(ready, 1))
    for a in ALONG_Z:
        help_on(a)
    start_x(ORDER[FIRST:])
    pass_on(1)
    pass_on(2)
    pass_on(3)

    @pl.loop(1, ROWS - 1)
    def _(a):
        density_row(far, a, None, dn.at[far, a])

    receive_pair(edges_d)


    def near_step(a):
        arrive(a)
        value_row(near, a, hv.at[a])
        finish_far(a)

    @pl.loop(1, ROWS // 2)
    def _(a):
        pl.when(a + 3 <= ALONG_Y[-1])(lambda: pass_on(a + 3))
        pl.when(a + 3 == DOWN_Y[-1])(lambda: pass_on(a + 3, top))
        near_step(a)

        @pl.when(a > 1)
        def _():
            near_density(a - 1)

    receive_pair(edges_n)

    @pl.loop(0, 2)
    def _(i):
        a = i * (ROWS - 1)
        density_row(far, a, None, dn.at[far, a])
        finish_far(a)

    near_density(0)

    @pl.loop(ROWS // 2, LAST)
    def _(a):
        near_step(a)
        near_density(a - 1)

    middle = TILES // 2
    for half, (first, stop, inner_first, inner_stop) in enumerate(
        ((0, middle, 0, middle - 1), (middle, TILES, middle - 1, TILES))
    ):
        for copy in x_halves(half):
            copy.wait_recv()
        value_row(near, LAST, hv.at[LAST], first=first, stop=stop)
        finish_far(LAST, first, stop)
        near_density(LAST - 1, first=first, stop=stop)
        near_density(LAST, first=inner_first, stop=inner_stop)
        near_density(LAST + 1, first=first, stop=stop)

    for pair in (edges_v, edges_d, edges_n):
        sent_pair(pair)
    for copy in mass_copies:
        copy.wait_send()

    @pl.loop(0, LAST)
    def _(a):
        for copy in x_copies(a):
            copy.wait_send()

    for copy in x_copies(ROWS - 1) + tuple(x_halves(0) + x_halves(1)):
        copy.wait_send()

    @pl.when(at_end)
    def _():
        for a in ALONG_Y:
            second_leg(0, a, twin).wait_send()

    pl.when(top)(lambda: second_leg(0, DOWN_Y[-1], twin).wait_send())

    for a in ALONG_Z:
        pl.when(helps_with(a))(lambda: second_leg(0, a, helped_to).wait_send())


def store(n, dn, value_out, density_out, sem):
    copies = []
    for k, (source, target) in enumerate(((n.at[:, pl.ds(1, ROWS)], value_out), (dn, density_out))):
        for r in range(2):
            copies.append(pltpu.make_async_copy(source.at[r], target.at[r], sem.at[2 * k + r]))
    for copy in copies:
        copy.start()
    for copy in copies:
        copy.wait()


def body(value_next, density):
    shape = (2, ROWS, GRID_V, NY)
    haloed = pltpu.VMEM((2, ROWS + 2, GRID_V, NY), F32)
    slab = pltpu.VMEM((ROWS, GRID_V, NY), F32)
    dma = pltpu.SemaphoreType.DMA
    n, dn = pl.pallas_call(
        kernel,
        out_shape=[pltpu.VMEM((2, ROWS + 2, GRID_V, NY), F32), pltpu.VMEM(shape, F32)],
        in_specs=[pl.BlockSpec(memory_space=pltpu.HBM)] * 2,
        out_specs=[pl.BlockSpec(memory_space=pltpu.VMEM)] * 2,
        scratch_shapes=[
            haloed, haloed, slab, slab,
            pltpu.VMEM((VEL, TILE, NY), F32), pltpu.VMEM((2, TILE, NY), F32),
            pltpu.VMEM((ALONG_Z[-1], GRID_V, NY), F32),
            dma((2,)), dma((3, 2)), dma((3, 2)), dma((VEL,)), dma((VEL,)),
            dma((2, ROWS + 1)), dma((2, ROWS + 1)), dma((ALONG_Z[-1],)), dma((ALONG_Z[-1],)), pltpu.SemaphoreType.REGULAR,
        ],
        compiler_params=pltpu.CompilerParams(
            collective_id=0, has_side_effects=True, vmem_limit_bytes=52 << 20
        ),
    )(value_next, density)
    return pl.pallas_call(
        store,
        out_shape=[jax.ShapeDtypeStruct(shape, F32)] * 2,
        in_specs=[pl.BlockSpec(memory_space=pltpu.VMEM)] * 2,
        out_specs=[pl.BlockSpec(memory_space=pl.ANY)] * 2,
        scratch_shapes=[dma((4,))],
        compiler_params=pltpu.CompilerParams(vmem_limit_bytes=32 << 20),
    )(n, dn)


def solution(mesh):
    spec = P("pos", "vel", None, None)
    return jax.shard_map(body, mesh=mesh, in_specs=(spec, spec), out_specs=(spec, spec), check_vma=False)
```

```python
import functools

import jax
import jax.numpy as jnp
from jax import lax
from jax.experimental import pallas as pl
from jax.experimental.pallas import tpu as pltpu
from jax.sharding import PartitionSpec as P

MESH = pl.DeviceIdType.MESH
COURANT = 0.4
CROWDING = 0.3
ROWS = 16
GRID_V = 64
NY = 512
TILE = 8
TILES = GRID_V // TILE
VEL = 4
POS = 32
F32 = jnp.float32
ALONG_Y = (1, 2, 3, 4)
DOWN_Y = (1, 2, 3, 4, 5)
ALONG_Z = (7, 8)
NEXT_Z = (7,)

LAST = ROWS - 2
ORDER = (7, 8, 0, ROWS - 1, 1, 2, 3, 4, 5, 6, *range(9, ROWS - 1))
LATE_ORDER = (0, ROWS - 1, 1, 2, 3, 4, 5, 6, *range(9, ROWS - 1))

FIRST = 10


def tile(t):
    return pl.ds(t * TILE, TILE)


def sublane():
    return lax.broadcasted_iota(jnp.int32, (TILE, NY), 0)


def speed_b(t):
    index = (sublane() + t * TILE).astype(F32)
    return jnp.abs(COURANT * ((index + 0.5 - GRID_V / 2) / (GRID_V / 2)))


def value_slab(c_ref, up_ref, dn_ref, x_ref, crowd, speed_x, out_ref, first=0, stop=TILES):
    place = sublane()

    def ahead(t):
        c = c_ref[tile(t), :]
        return c, pltpu.roll(c, TILE - 1, 0)

    begin = max(first - 1, 0)
    c, turned = ahead(begin)
    carried = jnp.zeros((TILE, NY), F32)
    for t in range(begin, stop):
        c_next, turned_next = ahead(t + 1) if t + 1 < TILES else (None, c)
        upper = jnp.where(place == TILE - 1, turned_next, turned) - c
        loss = pltpu.roll(upper * (1.2 + jnp.maximum(upper, 0.0)), 1, 0)
        if t >= first:
            gain = upper * (1.2 - jnp.minimum(upper, 0.0)) - jnp.where(place == 0, carried, loss)
            a_upper = up_ref[tile(t), :] - c
            a_lower = c - dn_ref[tile(t), :]
            gain = gain + a_upper * (1.2 - jnp.minimum(a_upper, 0.0))
            gain = gain - a_lower * (1.2 + jnp.maximum(a_lower, 0.0))
            y_next = pltpu.roll(c, 1 if t < TILES // 2 else NY - 1, 1)
            speed_y = speed_b(t)
            out = (1.0 - speed_x - speed_y) * c + speed_x * x_ref[tile(t), :] + speed_y * y_next
            out_ref[tile(t), :] = out + (0.125 * gain + crowd)
        carried = loss
        c, turned = c_next, turned_next


def density_slab(n_ref, n_up_ref, n_dn_ref, d_ref, d_up_ref, d_dn_ref, x_ref, speed_x, out_ref, first=0, stop=TILES):
    place = sublane()

    def ahead(t):
        d, n = d_ref[tile(t), :], n_ref[tile(t), :]
        return d, n, pltpu.roll(d, TILE - 1, 0), pltpu.roll(n, TILE - 1, 0)

    begin = max(first - 1, 0)
    d, n, d_turned, n_turned = ahead(begin)
    carried = jnp.zeros((TILE, NY), F32)
    for t in range(begin, stop):
        d_next, n_next, d_turned_next, n_turned_next = ahead(t + 1) if t + 1 < TILES else (None, None, d, n)
        last = place == TILE - 1
        d_beyond = jnp.where(last, d_turned_next, d_turned)
        step = n - jnp.where(last, n_turned_next, n_turned)
        flux = (jnp.maximum(step, 0.0) + 0.6) * (d - d_beyond) + step * d_beyond
        turned = pltpu.roll(flux, 1, 0)
        if t >= first:
            total = jnp.where(place == 0, carried, turned) - flux
            d_up, d_dn = d_up_ref[tile(t), :], d_dn_ref[tile(t), :]
            step = n - n_up_ref[tile(t), :]
            total = total - ((jnp.maximum(step, 0.0) + 0.6) * (d - d_up) + step * d_up)
            step = n_dn_ref[tile(t), :] - n
            total = total + ((jnp.maximum(step, 0.0) + 0.6) * (d_dn - d) + step * d)
            y_next = pltpu.roll(d, NY - 1 if t < TILES // 2 else 1, 1)
            speed_y = speed_b(t)
            out = (1.0 - speed_x - speed_y) * d + speed_y * y_next
            if x_ref is not None:
                out = out + speed_x * x_ref[tile(t), :]
            out_ref[tile(t), :] = out + 0.25 * total
        carried = turned
        d, n, d_turned, n_turned = d_next, n_next, d_turned_next, n_turned_next


def kernel(
    value, density, n, dn, v, d, hv, hd, crowd,
    mass, passing,
    load_sem, edge_send, edge_recv, mass_send, mass_recv, x_send, x_recv, pass_send, pass_recv, ready,
):
    vel, pos = lax.axis_index("vel"), lax.axis_index("pos")
    above, below = lax.rem(pos + 1, POS), lax.rem(pos + POS - 1, POS)
    low = vel < VEL // 2
    value_to = jnp.where(low, above, below)
    density_to = jnp.where(low, below, above)
    near = jnp.where(low, 0, 1)
    far = 1 - near
    has_lower, has_upper = vel > 0, vel < VEL - 1
    half = POS // 2
    place_x = lax.rem(pos, half)
    bottom, top = place_x == 0, place_x == half - 1
    at_end = jnp.logical_or(bottom, top)
    lower_top, upper_top = pos == half - 1, pos == POS - 1
    twin = lax.rem(pos + half, POS)
    other_end = jnp.where(bottom, pos + half - 1, pos - half + 1)
    high = jnp.logical_not(low)
    value_long = jnp.logical_or(jnp.logical_and(top, low), jnp.logical_and(bottom, high))
    density_long = jnp.logical_and(at_end, jnp.logical_not(value_long))
    up_1, down_1 = place_x == 3, place_x == 12
    up_2, down_2 = place_x == 7, place_x == 8
    any_1, any_2 = jnp.logical_or(up_1, down_1), jnp.logical_or(up_2, down_2)
    helper = jnp.logical_or(any_1, any_2)
    any_up = jnp.logical_or(up_1, up_2)
    reach = jnp.where(any_2, -4, 12)
    helped = jnp.where(any_up, pos + reach, pos - reach)
    helped_to = lax.rem(jnp.where(any_up, helped + 1, helped + POS - 1), POS)
    helps_value = jnp.logical_and(helper, jnp.where(any_up, low, high))
    via_z = jnp.where(bottom, pos + 12, jnp.where(top, pos - 12, jnp.where(up_1, pos + 4, pos - 4)))
    value_next_z = jnp.logical_and(any_1, helps_value)
    density_next_z = jnp.logical_and(any_1, jnp.logical_not(helps_value))

    barrier = pltpu.get_barrier_semaphore()

    def announce(**device):
        pl.semaphore_signal(barrier, inc=1, device_id=device, device_id_type=MESH)

    announce(pos=below)
    pl.when(jnp.logical_not(top))(lambda: announce(pos=above))
    for k in range(1, VEL):
        announce(vel=lax.rem(vel + k, VEL))

    @pl.when(bottom)
    def _():
        announce(pos=twin)
        announce(pos=other_end)

    pl.when(lower_top)(lambda: announce(pos=twin))
    pl.when(helper)(lambda: announce(pos=helped))
    pl.when(any_1)(lambda: announce(pos=helped_to))
    pl.when(place_x == 4)(lambda: announce(pos=pos + 3))
    pl.when(place_x == 11)(lambda: announce(pos=pos - 3))

    load_d = pltpu.make_async_copy(density, d.at[:, pl.ds(1, ROWS)], load_sem.at[0])
    load_v = pltpu.make_async_copy(value, v.at[:, pl.ds(1, ROWS)], load_sem.at[1])
    expected = jnp.where(bottom, 7, jnp.where(upper_top, 9, jnp.where(top, 8, jnp.where(helper, 6, 5))))
    pl.semaphore_wait(barrier, expected)

    def is_ready(**device):
        pl.semaphore_signal(ready, inc=1, device_id=device, device_id_type=MESH)

    @pl.when(top)
    def _():
        is_ready(pos=above)
        is_ready(pos=other_end)
        is_ready(pos=lax.rem(pos + 13, POS))

    pl.when(upper_top)(lambda: is_ready(pos=twin))
    pl.when(bottom)(lambda: is_ready(pos=lax.rem(pos + POS - 13, POS)))

    def x_copies(a):
        one = pl.ds(a, 1)
        return (
            pltpu.make_async_remote_copy(
                value.at[far, one], hv.at[one], x_send.at[0, a], x_recv.at[0, a],
                device_id={"pos": value_to}, device_id_type=MESH),
            pltpu.make_async_remote_copy(
                density.at[near, one], hd.at[one], x_send.at[1, a], x_recv.at[1, a],
                device_id={"pos": density_to}, device_id_type=MESH),
        )

    def x_halves(half):
        part = pl.ds(half * (GRID_V // 2), GRID_V // 2)
        return [
            pltpu.make_async_remote_copy(
                source.at[row, LAST, part], target.at[LAST, part], x_send.at[kind, LAST + 2 * half],
                x_recv.at[kind, LAST + 2 * half], device_id={"pos": to}, device_id_type=MESH)
            for kind, (source, row, target, to) in enumerate(
                ((value, far, hv, value_to), (density, near, hd, density_to)))
        ]

    def copies_of(a):
        return x_halves(0) + x_halves(1) if a == LAST else x_copies(a)

    def first_leg(kind, a, to):
        source = (value.at[far], density.at[near])[kind]
        return pltpu.make_async_remote_copy(
            source.at[pl.ds(a, 1)], passing.at[pl.ds(a - 1, 1)], x_send.at[kind, a], pass_recv.at[a - 1],
            device_id={"pos": to}, device_id_type=MESH)

    def second_leg(kind, a, to):
        return pltpu.make_async_remote_copy(
            passing.at[pl.ds(a - 1, 1)], (hv, hd)[kind].at[pl.ds(a, 1)], pass_send.at[a - 1], x_recv.at[kind, a],
            device_id={"pos": to}, device_id_type=MESH)

    def start_crossing(kind, a, passed=ALONG_Y):
        if a in passed:
            first_leg(kind, a, other_end).start()
        else:
            for copy in copies_of(a)[kind::2]:
                copy.start()

    special = jnp.logical_or(at_end, any_1)

    def start_x(rows):
        @pl.when(jnp.logical_not(special))
        def _():
            for a in rows:
                for copy in copies_of(a):
                    copy.start()

        for kind, (crosses, turns) in enumerate(((value_long, value_next_z), (density_long, density_next_z))):
            @pl.when(jnp.logical_and(special, jnp.logical_not(jnp.logical_or(crosses, turns))))
            def _():
                for a in rows:
                    for copy in copies_of(a)[kind::2]:
                        copy.start()

            @pl.when(turns)
            def _():
                for a in rows:
                    if a in NEXT_Z:
                        first_leg(kind, a, via_z).start()
                    else:
                        for copy in copies_of(a)[kind::2]:
                            copy.start()

            @pl.when(crosses)
            def _():
                for a in rows:
                    if a in ALONG_Z:
                        first_leg(kind, a, via_z).start()

            @pl.when(jnp.logical_and(crosses, top))
            def _():
                for a in rows:
                    if a not in ALONG_Z:
                        start_crossing(kind, a)

    def start_x_late():
        for kind, crosses in enumerate((value_long, density_long)):
            @pl.when(jnp.logical_and(crosses, bottom))
            def _():
                for a in LATE_ORDER:
                    start_crossing(kind, a, DOWN_Y)

    def pass_on(a, where=at_end):
        @pl.when(where)
        def _():
            first_leg(0, a, other_end).wait_recv()
            pl.when(density_long)(lambda: second_leg(0, a, twin).start())
            pl.when(value_long)(lambda: second_leg(1, a, twin).start())

    def helps_with(a):
        return helper if a in NEXT_Z else any_1

    def help_on(a):
        @pl.when(helps_with(a))
        def _():
            first_leg(0, a, helped).wait_recv()
            pl.when(helps_value)(lambda: second_leg(0, a, helped_to).start())
            pl.when(jnp.logical_not(helps_value))(lambda: second_leg(1, a, helped_to).start())

    def edge_copies(k, source, target):
        to_upper = pltpu.make_async_remote_copy(
            source.at[:, pl.ds(ROWS - 1, 1)], target.at[:, pl.ds(0, 1)], edge_send.at[k, 0], edge_recv.at[k, 0],
            device_id={"vel": lax.rem(vel + 1, VEL)}, device_id_type=MESH)
        to_lower = pltpu.make_async_remote_copy(
            source.at[:, pl.ds(0, 1)], target.at[:, pl.ds(ROWS + 1, 1)], edge_send.at[k, 1], edge_recv.at[k, 1],
            device_id={"vel": lax.rem(vel + VEL - 1, VEL)}, device_id_type=MESH)
        return to_upper, to_lower

    def start_pair(pair):
        to_upper, to_lower = pair

        @pl.when(has_upper)
        def _():
            to_upper.start()

        @pl.when(has_lower)
        def _():
            to_lower.start()

    def receive_pair(pair):
        to_upper, to_lower = pair

        @pl.when(has_lower)
        def _():
            to_upper.wait_recv()

        @pl.when(has_upper)
        def _():
            to_lower.wait_recv()

    def sent_pair(pair):
        to_upper, to_lower = pair

        @pl.when(has_upper)
        def _():
            to_upper.wait_send()

        @pl.when(has_lower)
        def _():
            to_lower.wait_send()

    edges_v, edges_d = edge_copies(0, value, v), edge_copies(1, density, d)
    start_x(ORDER[:1])
    start_pair(edges_v)
    load_d.start()
    load_v.start()
    start_x(ORDER[1:3])
    start_pair(edges_d)
    start_x(ORDER[3:FIRST])

    load_d.wait()
    place = sublane()

    def add_row(i, sums):
        parts = []
        for r in range(2):
            total = sums[r]
            for t in range(TILES):
                total = total + d[r, i + 1, tile(t), :]
            parts.append(total)
        return tuple(parts)

    zero = jnp.zeros((TILE, NY), F32)
    sums = lax.fori_loop(0, ROWS, add_row, (zero, zero))
    sums = [jnp.sum(s, axis=0, keepdims=True) for s in sums]
    mass[vel] = jnp.where(place == 0, sums[0], sums[1])
    mass_copies = [
        pltpu.make_async_remote_copy(
            mass.at[vel], mass.at[vel], mass_send.at[k], mass_recv.at[k],
            device_id={"vel": lax.rem(vel + k, VEL)}, device_id_type=MESH)
        for k in range(1, VEL)
    ]
    for copy in mass_copies:
        copy.start()
    pl.when(bottom)(lambda: pl.semaphore_wait(ready, 2))
    start_x_late()
    load_v.wait()

    def repeat_edges(field, rows):
        @pl.when(jnp.logical_not(has_lower))
        def _():
            for r in rows:
                field[r, 0] = field[r, 1]

        @pl.when(jnp.logical_not(has_upper))
        def _():
            for r in rows:
                field[r, ROWS + 1] = field[r, ROWS]

    repeat_edges(v, (0, 1))
    repeat_edges(d, (0, 1))
    for copy in mass_copies:
        copy.wait_recv()
    total = (mass[0] + mass[1]) + (mass[2] + mass[3])
    total = total / (GRID_V * GRID_V)
    total = CROWDING * total * total
    crowd[0] = jnp.broadcast_to(total[0:1], (TILE, NY))
    crowd[1] = jnp.broadcast_to(total[1:2], (TILE, NY))

    def speed_a(a):
        index = (vel * ROWS + a).astype(F32)
        return jnp.abs(COURANT * ((index + 0.5 - GRID_V / 2) / (GRID_V / 2)))

    def value_row(row, a, x_ref, **tiles):
        value_slab(v.at[row, a + 1], v.at[row, a + 2], v.at[row, a], x_ref, crowd[row], speed_a(a), n.at[row, a + 1], **tiles)

    def density_row(row, a, x_ref, out_ref, **tiles):
        density_slab(
            n.at[row, a + 1], n.at[row, a + 2], n.at[row, a],
            d.at[row, a + 1], d.at[row, a + 2], d.at[row, a], x_ref, speed_a(a), out_ref, **tiles)

    def arrive(a):
        for copy in x_copies(a):
            copy.wait_recv()

    def finish_far(a, first=0, stop=TILES):
        speed_x = speed_a(a)
        for t in range(first, stop):
            dn[far, a, tile(t), :] = dn[far, a, tile(t), :] + speed_x * hd[a, tile(t), :]

    def near_density(a, **tiles):
        density_row(near, a, d.at[far, a + 1], dn.at[near, a], **tiles)

    def inner_values(here):
        @pl.loop(jnp.where(here, 1, ROWS - 1), ROWS - 1)
        def _(a):
            value_row(far, a, v.at[near, a + 1])

    inner_values(at_end)

    receive_pair(edges_v)

    @pl.loop(0, 2)
    def _(i):
        a = i * (ROWS - 1)
        arrive(a)
        value_row(far, a, v.at[near, a + 1])
        value_row(near, a, hv.at[a])

    edges_n = edge_copies(2, n.at[:, pl.ds(1, ROWS)], n)
    start_pair(edges_n)
    repeat_edges(n, (0, 1))
    inner_values(jnp.logical_not(at_end))
    pl.when(jnp.logical_or(lower_top, any_1))(lambda: pl.semaphore_wait(ready, 1))
    for a in ALONG_Z:
        help_on(a)
    start_x(ORDER[FIRST:])
    pass_on(1)
    pass_on(2)
    pass_on(3)

    @pl.loop(1, ROWS - 1)
    def _(a):
        density_row(far, a, None, dn.at[far, a])

    receive_pair(edges_d)


    def near_step(a):
        arrive(a)
        value_row(near, a, hv.at[a])
        finish_far(a)

    @pl.loop(1, ROWS // 2)
    def _(a):
        pl.when(a + 3 <= ALONG_Y[-1])(lambda: pass_on(a + 3))
        pl.when(a + 3 == DOWN_Y[-1])(lambda: pass_on(a + 3, top))
        near_step(a)

        @pl.when(a > 1)
        def _():
            near_density(a - 1)

    receive_pair(edges_n)

    @pl.loop(0, 2)
    def _(i):
        a = i * (ROWS - 1)
        density_row(far, a, None, dn.at[far, a])
        finish_far(a)

    near_density(0)

    @pl.loop(ROWS // 2, LAST)
    def _(a):
        near_step(a)
        near_density(a - 1)

    for copy in x_halves(0) + x_halves(1):
        copy.wait_recv()

    for pair in (edges_v, edges_d, edges_n):
        sent_pair(pair)
    for copy in mass_copies:
        copy.wait_send()

    @pl.loop(0, LAST)
    def _(a):
        for copy in x_copies(a):
            copy.wait_send()

    for copy in x_copies(ROWS - 1) + tuple(x_halves(0) + x_halves(1)):
        copy.wait_send()

    @pl.when(at_end)
    def _():
        for a in ALONG_Y:
            second_leg(0, a, twin).wait_send()

    pl.when(top)(lambda: second_leg(0, DOWN_Y[-1], twin).wait_send())

    for a in ALONG_Z:
        pl.when(helps_with(a))(lambda: second_leg(0, a, helped_to).wait_send())


def store(n, dn, v, d, hv, hd, crowd, value_out, density_out, last_value, last_density, last_far, sem):
    vel = lax.axis_index("vel")
    near = jnp.where(vel < VEL // 2, 0, 1)
    far = 1 - near
    count = [0]

    def copy(source, target):
        made = pltpu.make_async_copy(source, target, sem.at[count[0]])
        count[0] += 1
        made.start()
        return made

    def rows(first, stop):
        return pl.ds(first, stop - first)

    copies = [
        copy(n.at[far, rows(1, ROWS + 1)], value_out.at[far]),
        copy(n.at[near, rows(1, LAST + 1)], value_out.at[near, rows(0, LAST)]),
        copy(dn.at[far, rows(0, LAST)], density_out.at[far, rows(0, LAST)]),
        copy(dn.at[near, rows(0, LAST - 1)], density_out.at[near, rows(0, LAST - 1)]),
        copy(n.at[near, rows(LAST + 2, ROWS + 1)], value_out.at[near, rows(LAST + 1, ROWS)]),
        copy(dn.at[far, rows(LAST + 1, ROWS)], density_out.at[far, rows(LAST + 1, ROWS)]),
    ]

    def speed(a):
        index = (vel * ROWS + a).astype(F32)
        return jnp.abs(COURANT * ((index + 0.5 - GRID_V / 2) / (GRID_V / 2)))

    for t in range(TILES):
        last_far[0, tile(t), :] = dn[far, LAST, tile(t), :] + speed(LAST) * hd[LAST, tile(t), :]
    copies.append(copy(last_far, density_out.at[far, rows(LAST, LAST + 1)]))
    at = LAST + 1
    value_slab(
        v.at[near, at], v.at[near, at + 1], v.at[near, at - 1], hv.at[LAST], crowd[near], speed(LAST), last_value.at[0])
    copies.append(copy(last_value, value_out.at[near, rows(LAST, LAST + 1)]))
    levels = [n.at[near, at - 2], n.at[near, at - 1], last_value.at[0], n.at[near, at + 1], n.at[near, at + 2]]
    for k in range(3):
        here = at - 1 + k
        density_slab(
            levels[k + 1], levels[k + 2], levels[k], d.at[near, here], d.at[near, here + 1], d.at[near, here - 1],
            d.at[far, here], speed(here - 1), last_density.at[k])
    copies.append(copy(last_density, density_out.at[near, rows(LAST - 1, ROWS)]))
    for made in copies:
        made.wait()


def body(value_next, density):
    shape = (2, ROWS, GRID_V, NY)
    haloed = pltpu.VMEM((2, ROWS + 2, GRID_V, NY), F32)
    slab = pltpu.VMEM((ROWS, GRID_V, NY), F32)
    dma = pltpu.SemaphoreType.DMA
    held = pl.pallas_call(
        kernel,
        out_shape=[haloed, pltpu.VMEM(shape, F32), haloed, haloed, slab, slab, pltpu.VMEM((2, TILE, NY), F32)],
        in_specs=[pl.BlockSpec(memory_space=pltpu.HBM)] * 2,
        out_specs=[pl.BlockSpec(memory_space=pltpu.VMEM)] * 7,
        scratch_shapes=[
            pltpu.VMEM((VEL, TILE, NY), F32),
            pltpu.VMEM((ALONG_Z[-1], GRID_V, NY), F32),
            dma((2,)), dma((3, 2)), dma((3, 2)), dma((VEL,)), dma((VEL,)),
            dma((2, ROWS + 1)), dma((2, ROWS + 1)), dma((ALONG_Z[-1],)), dma((ALONG_Z[-1],)), pltpu.SemaphoreType.REGULAR,
        ],
        compiler_params=pltpu.CompilerParams(
            collective_id=0, has_side_effects=True, vmem_limit_bytes=40 << 20
        ),
    )(value_next, density)
    return pl.pallas_call(
        store,
        out_shape=[jax.ShapeDtypeStruct(shape, F32)] * 2,
        in_specs=[pl.BlockSpec(memory_space=pltpu.VMEM)] * 7,
        out_specs=[pl.BlockSpec(memory_space=pl.ANY)] * 2,
        scratch_shapes=[pltpu.VMEM((1, GRID_V, NY), F32), pltpu.VMEM((3, GRID_V, NY), F32), pltpu.VMEM((1, GRID_V, NY), F32), dma((9,))],
        compiler_params=pltpu.CompilerParams(vmem_limit_bytes=8 << 20),
    )(*held)


def solution(mesh):
    spec = P("pos", "vel", None, None)
    return jax.shard_map(body, mesh=mesh, in_specs=(spec, spec), out_specs=(spec, spec), check_vma=False)
```

```python
import functools

import jax
import jax.numpy as jnp
from jax import lax
from jax.experimental import pallas as pl
from jax.experimental.pallas import tpu as pltpu
from jax.sharding import PartitionSpec as P

MESH = pl.DeviceIdType.MESH
COURANT = 0.4
CROWDING = 0.3
ROWS = 16
GRID_V = 64
NY = 512
TILE = 8
TILES = GRID_V // TILE
VEL = 4
POS = 32
F32 = jnp.float32
ALONG_Y = (1, 2, 3, 4)
DOWN_Y = (1, 2, 3, 4, 5)
ALONG_Z = (7, 8)
NEXT_Z = (7,)

LAST = ROWS - 2
ORDER = (7, 8, 0, ROWS - 1, 1, 2, 3, 4, 5, 6, *range(9, ROWS - 1))
LATE_ORDER = (0, ROWS - 1, 1, 2, 3, 4, 5, 6, *range(9, ROWS - 1))

FIRST = 12


def tile(t):
    return pl.ds(t * TILE, TILE)


def sublane():
    return lax.broadcasted_iota(jnp.int32, (TILE, NY), 0)


def speed_b(t):
    index = (sublane() + t * TILE).astype(F32)
    return jnp.abs(COURANT * ((index + 0.5 - GRID_V / 2) / (GRID_V / 2)))


def value_slab(c_ref, up_ref, dn_ref, x_ref, crowd, speed_x, out_ref, first=0, stop=TILES):
    place = sublane()

    def ahead(t):
        c = c_ref[tile(t), :]
        return c, pltpu.roll(c, TILE - 1, 0)

    begin = max(first - 1, 0)
    c, turned = ahead(begin)
    carried = jnp.zeros((TILE, NY), F32)
    for t in range(begin, stop):
        c_next, turned_next = ahead(t + 1) if t + 1 < TILES else (None, c)
        upper = jnp.where(place == TILE - 1, turned_next, turned) - c
        loss = pltpu.roll(upper * (1.2 + jnp.maximum(upper, 0.0)), 1, 0)
        if t >= first:
            gain = upper * (1.2 - jnp.minimum(upper, 0.0)) - jnp.where(place == 0, carried, loss)
            a_upper = up_ref[tile(t), :] - c
            a_lower = c - dn_ref[tile(t), :]
            gain = gain + a_upper * (1.2 - jnp.minimum(a_upper, 0.0))
            gain = gain - a_lower * (1.2 + jnp.maximum(a_lower, 0.0))
            y_next = pltpu.roll(c, 1 if t < TILES // 2 else NY - 1, 1)
            speed_y = speed_b(t)
            out = (1.0 - speed_x - speed_y) * c + speed_x * x_ref[tile(t), :] + speed_y * y_next
            out_ref[tile(t), :] = out + (0.125 * gain + crowd)
        carried = loss
        c, turned = c_next, turned_next


def density_slab(n_ref, n_up_ref, n_dn_ref, d_ref, d_up_ref, d_dn_ref, x_ref, speed_x, out_ref, first=0, stop=TILES):
    place = sublane()

    def ahead(t):
        d, n = d_ref[tile(t), :], n_ref[tile(t), :]
        return d, n, pltpu.roll(d, TILE - 1, 0), pltpu.roll(n, TILE - 1, 0)

    begin = max(first - 1, 0)
    d, n, d_turned, n_turned = ahead(begin)
    carried = jnp.zeros((TILE, NY), F32)
    for t in range(begin, stop):
        d_next, n_next, d_turned_next, n_turned_next = ahead(t + 1) if t + 1 < TILES else (None, None, d, n)
        last = place == TILE - 1
        d_beyond = jnp.where(last, d_turned_next, d_turned)
        step = n - jnp.where(last, n_turned_next, n_turned)
        flux = (jnp.maximum(step, 0.0) + 0.6) * (d - d_beyond) + step * d_beyond
        turned = pltpu.roll(flux, 1, 0)
        if t >= first:
            total = jnp.where(place == 0, carried, turned) - flux
            d_up, d_dn = d_up_ref[tile(t), :], d_dn_ref[tile(t), :]
            step = n - n_up_ref[tile(t), :]
            total = total - ((jnp.maximum(step, 0.0) + 0.6) * (d - d_up) + step * d_up)
            step = n_dn_ref[tile(t), :] - n
            total = total + ((jnp.maximum(step, 0.0) + 0.6) * (d_dn - d) + step * d)
            y_next = pltpu.roll(d, NY - 1 if t < TILES // 2 else 1, 1)
            speed_y = speed_b(t)
            out = (1.0 - speed_x - speed_y) * d + speed_y * y_next
            if x_ref is not None:
                out = out + speed_x * x_ref[tile(t), :]
            out_ref[tile(t), :] = out + 0.25 * total
        carried = turned
        d, n, d_turned, n_turned = d_next, n_next, d_turned_next, n_turned_next


def kernel(
    value, density, n, dn, v, d, hv, hd, crowd,
    mass, passing,
    load_sem, edge_send, edge_recv, mass_send, mass_recv, x_send, x_recv, pass_send, pass_recv, ready,
):
    vel, pos = lax.axis_index("vel"), lax.axis_index("pos")
    above, below = lax.rem(pos + 1, POS), lax.rem(pos + POS - 1, POS)
    low = vel < VEL // 2
    value_to = jnp.where(low, above, below)
    density_to = jnp.where(low, below, above)
    near = jnp.where(low, 0, 1)
    far = 1 - near
    has_lower, has_upper = vel > 0, vel < VEL - 1
    half = POS // 2
    place_x = lax.rem(pos, half)
    bottom, top = place_x == 0, place_x == half - 1
    at_end = jnp.logical_or(bottom, top)
    lower_top, upper_top = pos == half - 1, pos == POS - 1
    twin = lax.rem(pos + half, POS)
    other_end = jnp.where(bottom, pos + half - 1, pos - half + 1)
    high = jnp.logical_not(low)
    value_long = jnp.logical_or(jnp.logical_and(top, low), jnp.logical_and(bottom, high))
    density_long = jnp.logical_and(at_end, jnp.logical_not(value_long))
    up_1, down_1 = place_x == 3, place_x == 12
    up_2, down_2 = place_x == 7, place_x == 8
    any_1, any_2 = jnp.logical_or(up_1, down_1), jnp.logical_or(up_2, down_2)
    helper = jnp.logical_or(any_1, any_2)
    any_up = jnp.logical_or(up_1, up_2)
    reach = jnp.where(any_2, -4, 12)
    helped = jnp.where(any_up, pos + reach, pos - reach)
    helped_to = lax.rem(jnp.where(any_up, helped + 1, helped + POS - 1), POS)
    helps_value = jnp.logical_and(helper, jnp.where(any_up, low, high))
    via_z = jnp.where(bottom, pos + 12, jnp.where(top, pos - 12, jnp.where(up_1, pos + 4, pos - 4)))
    value_next_z = jnp.logical_and(any_1, helps_value)
    density_next_z = jnp.logical_and(any_1, jnp.logical_not(helps_value))

    barrier = pltpu.get_barrier_semaphore()

    def announce(**device):
        pl.semaphore_signal(barrier, inc=1, device_id=device, device_id_type=MESH)

    announce(pos=below)
    pl.when(jnp.logical_not(top))(lambda: announce(pos=above))
    for k in range(1, VEL):
        announce(vel=lax.rem(vel + k, VEL))

    @pl.when(bottom)
    def _():
        announce(pos=twin)
        announce(pos=other_end)

    pl.when(lower_top)(lambda: announce(pos=twin))
    pl.when(helper)(lambda: announce(pos=helped))
    pl.when(any_1)(lambda: announce(pos=helped_to))
    pl.when(place_x == 4)(lambda: announce(pos=pos + 3))
    pl.when(place_x == 11)(lambda: announce(pos=pos - 3))

    load_d = pltpu.make_async_copy(density, d.at[:, pl.ds(1, ROWS)], load_sem.at[0])
    load_v = pltpu.make_async_copy(value, v.at[:, pl.ds(1, ROWS)], load_sem.at[1])
    expected = jnp.where(bottom, 7, jnp.where(upper_top, 9, jnp.where(top, 8, jnp.where(helper, 6, 5))))
    pl.semaphore_wait(barrier, expected)

    def is_ready(**device):
        pl.semaphore_signal(ready, inc=1, device_id=device, device_id_type=MESH)

    @pl.when(top)
    def _():
        is_ready(pos=above)
        is_ready(pos=other_end)
        is_ready(pos=lax.rem(pos + 13, POS))

    pl.when(upper_top)(lambda: is_ready(pos=twin))
    pl.when(bottom)(lambda: is_ready(pos=lax.rem(pos + POS - 13, POS)))

    def x_copies(a):
        one = pl.ds(a, 1)
        return (
            pltpu.make_async_remote_copy(
                value.at[far, one], hv.at[one], x_send.at[0, a], x_recv.at[0, a],
                device_id={"pos": value_to}, device_id_type=MESH),
            pltpu.make_async_remote_copy(
                density.at[near, one], hd.at[one], x_send.at[1, a], x_recv.at[1, a],
                device_id={"pos": density_to}, device_id_type=MESH),
        )

    def x_halves(half):
        part = pl.ds(half * (GRID_V // 2), GRID_V // 2)
        return [
            pltpu.make_async_remote_copy(
                source.at[row, LAST, part], target.at[LAST, part], x_send.at[kind, LAST + 2 * half],
                x_recv.at[kind, LAST + 2 * half], device_id={"pos": to}, device_id_type=MESH)
            for kind, (source, row, target, to) in enumerate(
                ((value, far, hv, value_to), (density, near, hd, density_to)))
        ]

    def copies_of(a):
        return x_halves(0) + x_halves(1) if a == LAST else x_copies(a)

    def first_leg(kind, a, to):
        source = (value.at[far], density.at[near])[kind]
        return pltpu.make_async_remote_copy(
            source.at[pl.ds(a, 1)], passing.at[pl.ds(a - 1, 1)], x_send.at[kind, a], pass_recv.at[a - 1],
            device_id={"pos": to}, device_id_type=MESH)

    def second_leg(kind, a, to):
        return pltpu.make_async_remote_copy(
            passing.at[pl.ds(a - 1, 1)], (hv, hd)[kind].at[pl.ds(a, 1)], pass_send.at[a - 1], x_recv.at[kind, a],
            device_id={"pos": to}, device_id_type=MESH)

    def start_crossing(kind, a, passed=ALONG_Y):
        if a in passed:
            first_leg(kind, a, other_end).start()
        else:
            for copy in copies_of(a)[kind::2]:
                copy.start()

    special = jnp.logical_or(at_end, any_1)

    def start_x(rows):
        @pl.when(jnp.logical_not(special))
        def _():
            for a in rows:
                for copy in copies_of(a):
                    copy.start()

        for kind, (crosses, turns) in enumerate(((value_long, value_next_z), (density_long, density_next_z))):
            @pl.when(jnp.logical_and(special, jnp.logical_not(jnp.logical_or(crosses, turns))))
            def _():
                for a in rows:
                    for copy in copies_of(a)[kind::2]:
                        copy.start()

            @pl.when(turns)
            def _():
                for a in rows:
                    if a in NEXT_Z:
                        first_leg(kind, a, via_z).start()
                    else:
                        for copy in copies_of(a)[kind::2]:
                            copy.start()

            @pl.when(crosses)
            def _():
                for a in rows:
                    if a in ALONG_Z:
                        first_leg(kind, a, via_z).start()

            @pl.when(jnp.logical_and(crosses, top))
            def _():
                for a in rows:
                    if a not in ALONG_Z:
                        start_crossing(kind, a)

    def start_x_late():
        for kind, crosses in enumerate((value_long, density_long)):
            @pl.when(jnp.logical_and(crosses, bottom))
            def _():
                for a in LATE_ORDER:
                    start_crossing(kind, a, DOWN_Y)

    def pass_on(a, where=at_end):
        @pl.when(where)
        def _():
            first_leg(0, a, other_end).wait_recv()
            pl.when(density_long)(lambda: second_leg(0, a, twin).start())
            pl.when(value_long)(lambda: second_leg(1, a, twin).start())

    def helps_with(a):
        return helper if a in NEXT_Z else any_1

    def help_on(a):
        @pl.when(helps_with(a))
        def _():
            first_leg(0, a, helped).wait_recv()
            pl.when(helps_value)(lambda: second_leg(0, a, helped_to).start())
            pl.when(jnp.logical_not(helps_value))(lambda: second_leg(1, a, helped_to).start())

    def edge_copies(k, source, target):
        to_upper = pltpu.make_async_remote_copy(
            source.at[:, pl.ds(ROWS - 1, 1)], target.at[:, pl.ds(0, 1)], edge_send.at[k, 0], edge_recv.at[k, 0],
            device_id={"vel": lax.rem(vel + 1, VEL)}, device_id_type=MESH)
        to_lower = pltpu.make_async_remote_copy(
            source.at[:, pl.ds(0, 1)], target.at[:, pl.ds(ROWS + 1, 1)], edge_send.at[k, 1], edge_recv.at[k, 1],
            device_id={"vel": lax.rem(vel + VEL - 1, VEL)}, device_id_type=MESH)
        return to_upper, to_lower

    def start_pair(pair):
        to_upper, to_lower = pair

        @pl.when(has_upper)
        def _():
            to_upper.start()

        @pl.when(has_lower)
        def _():
            to_lower.start()

    def receive_pair(pair):
        to_upper, to_lower = pair

        @pl.when(has_lower)
        def _():
            to_upper.wait_recv()

        @pl.when(has_upper)
        def _():
            to_lower.wait_recv()

    def sent_pair(pair):
        to_upper, to_lower = pair

        @pl.when(has_upper)
        def _():
            to_upper.wait_send()

        @pl.when(has_lower)
        def _():
            to_lower.wait_send()

    edges_v, edges_d = edge_copies(0, value, v), edge_copies(1, density, d)
    start_x(ORDER[:1])
    start_pair(edges_v)
    load_d.start()
    load_v.start()
    start_x(ORDER[1:3])
    start_pair(edges_d)
    start_x(ORDER[3:FIRST])

    load_d.wait()
    place = sublane()

    def add_row(i, sums):
        parts = []
        for r in range(2):
            total = sums[r]
            for t in range(TILES):
                total = total + d[r, i + 1, tile(t), :]
            parts.append(total)
        return tuple(parts)

    zero = jnp.zeros((TILE, NY), F32)
    sums = lax.fori_loop(0, ROWS, add_row, (zero, zero))
    sums = [jnp.sum(s, axis=0, keepdims=True) for s in sums]
    mass[vel] = jnp.where(place == 0, sums[0], sums[1])
    mass_copies = [
        pltpu.make_async_remote_copy(
            mass.at[vel], mass.at[vel], mass_send.at[k], mass_recv.at[k],
            device_id={"vel": lax.rem(vel + k, VEL)}, device_id_type=MESH)
        for k in range(1, VEL)
    ]
    for copy in mass_copies:
        copy.start()
    pl.when(bottom)(lambda: pl.semaphore_wait(ready, 2))
    start_x_late()
    load_v.wait()

    def repeat_edges(field, rows):
        @pl.when(jnp.logical_not(has_lower))
        def _():
            for r in rows:
                field[r, 0] = field[r, 1]

        @pl.when(jnp.logical_not(has_upper))
        def _():
            for r in rows:
                field[r, ROWS + 1] = field[r, ROWS]

    repeat_edges(v, (0, 1))
    repeat_edges(d, (0, 1))
    for copy in mass_copies:
        copy.wait_recv()
    total = (mass[0] + mass[1]) + (mass[2] + mass[3])
    total = total / (GRID_V * GRID_V)
    total = CROWDING * total * total
    crowd[0] = jnp.broadcast_to(total[0:1], (TILE, NY))
    crowd[1] = jnp.broadcast_to(total[1:2], (TILE, NY))

    def speed_a(a):
        index = (vel * ROWS + a).astype(F32)
        return jnp.abs(COURANT * ((index + 0.5 - GRID_V / 2) / (GRID_V / 2)))

    def value_row(row, a, x_ref, **tiles):
        value_slab(v.at[row, a + 1], v.at[row, a + 2], v.at[row, a], x_ref, crowd[row], speed_a(a), n.at[row, a + 1], **tiles)

    def density_row(row, a, x_ref, out_ref, **tiles):
        density_slab(
            n.at[row, a + 1], n.at[row, a + 2], n.at[row, a],
            d.at[row, a + 1], d.at[row, a + 2], d.at[row, a], x_ref, speed_a(a), out_ref, **tiles)

    def arrive(a):
        for copy in x_copies(a):
            copy.wait_recv()

    def finish_far(a, first=0, stop=TILES):
        speed_x = speed_a(a)
        for t in range(first, stop):
            dn[far, a, tile(t), :] = dn[far, a, tile(t), :] + speed_x * hd[a, tile(t), :]

    def near_density(a, **tiles):
        density_row(near, a, d.at[far, a + 1], dn.at[near, a], **tiles)

    def inner_values(here):
        @pl.loop(jnp.where(here, 1, ROWS - 1), ROWS - 1)
        def _(a):
            value_row(far, a, v.at[near, a + 1])

    inner_values(at_end)

    receive_pair(edges_v)

    @pl.loop(0, 2)
    def _(i):
        a = i * (ROWS - 1)
        arrive(a)
        value_row(far, a, v.at[near, a + 1])
        value_row(near, a, hv.at[a])

    edges_n = edge_copies(2, n.at[:, pl.ds(1, ROWS)], n)
    start_pair(edges_n)
    repeat_edges(n, (0, 1))
    inner_values(jnp.logical_not(at_end))
    pl.when(jnp.logical_or(lower_top, any_1))(lambda: pl.semaphore_wait(ready, 1))
    for a in ALONG_Z:
        help_on(a)
    start_x(ORDER[FIRST:])
    pass_on(1)
    pass_on(2)
    pass_on(3)

    @pl.loop(1, ROWS - 1)
    def _(a):
        density_row(far, a, None, dn.at[far, a])

    receive_pair(edges_d)


    def near_step(a):
        arrive(a)
        value_row(near, a, hv.at[a])
        finish_far(a)

    @pl.loop(1, ROWS // 2)
    def _(a):
        pl.when(a + 3 <= ALONG_Y[-1])(lambda: pass_on(a + 3))
        pl.when(a + 3 == DOWN_Y[-1])(lambda: pass_on(a + 3, top))
        near_step(a)

        @pl.when(a > 1)
        def _():
            near_density(a - 1)

    receive_pair(edges_n)

    @pl.loop(0, 2)
    def _(i):
        a = i * (ROWS - 1)
        density_row(far, a, None, dn.at[far, a])
        finish_far(a)

    near_density(0)

    @pl.loop(ROWS // 2, LAST)
    def _(a):
        near_step(a)
        near_density(a - 1)

    for copy in x_halves(0) + x_halves(1):
        copy.wait_recv()

    for pair in (edges_v, edges_d, edges_n):
        sent_pair(pair)
    for copy in mass_copies:
        copy.wait_send()

    @pl.loop(0, LAST)
    def _(a):
        for copy in x_copies(a):
            copy.wait_send()

    for copy in x_copies(ROWS - 1) + tuple(x_halves(0) + x_halves(1)):
        copy.wait_send()

    @pl.when(at_end)
    def _():
        for a in ALONG_Y:
            second_leg(0, a, twin).wait_send()

    pl.when(top)(lambda: second_leg(0, DOWN_Y[-1], twin).wait_send())

    for a in ALONG_Z:
        pl.when(helps_with(a))(lambda: second_leg(0, a, helped_to).wait_send())


def store(n, dn, v, d, hv, hd, crowd, value_out, density_out, last_value, last_density, last_far, sem):
    vel = lax.axis_index("vel")
    near = jnp.where(vel < VEL // 2, 0, 1)
    far = 1 - near
    count = [0]

    def copy(source, target):
        made = pltpu.make_async_copy(source, target, sem.at[count[0]])
        count[0] += 1
        made.start()
        return made

    def rows(first, stop):
        return pl.ds(first, stop - first)

    copies = [
        copy(n.at[far, rows(1, ROWS + 1)], value_out.at[far]),
        copy(n.at[near, rows(1, LAST + 1)], value_out.at[near, rows(0, LAST)]),
        copy(dn.at[far, rows(0, LAST)], density_out.at[far, rows(0, LAST)]),
        copy(dn.at[near, rows(0, LAST - 1)], density_out.at[near, rows(0, LAST - 1)]),
        copy(n.at[near, rows(LAST + 2, ROWS + 1)], value_out.at[near, rows(LAST + 1, ROWS)]),
        copy(dn.at[far, rows(LAST + 1, ROWS)], density_out.at[far, rows(LAST + 1, ROWS)]),
    ]

    def speed(a):
        index = (vel * ROWS + a).astype(F32)
        return jnp.abs(COURANT * ((index + 0.5 - GRID_V / 2) / (GRID_V / 2)))

    for t in range(TILES):
        last_far[0, tile(t), :] = dn[far, LAST, tile(t), :] + speed(LAST) * hd[LAST, tile(t), :]
    copies.append(copy(last_far, density_out.at[far, rows(LAST, LAST + 1)]))
    at = LAST + 1
    value_slab(
        v.at[near, at], v.at[near, at + 1], v.at[near, at - 1], hv.at[LAST], crowd[near], speed(LAST), last_value.at[0])
    copies.append(copy(last_value, value_out.at[near, rows(LAST, LAST + 1)]))
    levels = [n.at[near, at - 2], n.at[near, at - 1], last_value.at[0], n.at[near, at + 1], n.at[near, at + 2]]
    for k in range(3):
        here = at - 1 + k
        density_slab(
            levels[k + 1], levels[k + 2], levels[k], d.at[near, here], d.at[near, here + 1], d.at[near, here - 1],
            d.at[far, here], speed(here - 1), last_density.at[k])
    copies.append(copy(last_density, density_out.at[near, rows(LAST - 1, ROWS)]))
    for made in copies:
        made.wait()


def body(value_next, density):
    shape = (2, ROWS, GRID_V, NY)
    haloed = pltpu.VMEM((2, ROWS + 2, GRID_V, NY), F32)
    slab = pltpu.VMEM((ROWS, GRID_V, NY), F32)
    dma = pltpu.SemaphoreType.DMA
    held = pl.pallas_call(
        kernel,
        out_shape=[haloed, pltpu.VMEM(shape, F32), haloed, haloed, slab, slab, pltpu.VMEM((2, TILE, NY), F32)],
        in_specs=[pl.BlockSpec(memory_space=pltpu.HBM)] * 2,
        out_specs=[pl.BlockSpec(memory_space=pltpu.VMEM)] * 7,
        scratch_shapes=[
            pltpu.VMEM((VEL, TILE, NY), F32),
            pltpu.VMEM((ALONG_Z[-1], GRID_V, NY), F32),
            dma((2,)), dma((3, 2)), dma((3, 2)), dma((VEL,)), dma((VEL,)),
            dma((2, ROWS + 1)), dma((2, ROWS + 1)), dma((ALONG_Z[-1],)), dma((ALONG_Z[-1],)), pltpu.SemaphoreType.REGULAR,
        ],
        compiler_params=pltpu.CompilerParams(
            collective_id=0, has_side_effects=True, vmem_limit_bytes=40 << 20
        ),
    )(value_next, density)
    return pl.pallas_call(
        store,
        out_shape=[jax.ShapeDtypeStruct(shape, F32)] * 2,
        in_specs=[pl.BlockSpec(memory_space=pltpu.VMEM)] * 7,
        out_specs=[pl.BlockSpec(memory_space=pl.ANY)] * 2,
        scratch_shapes=[pltpu.VMEM((1, GRID_V, NY), F32), pltpu.VMEM((3, GRID_V, NY), F32), pltpu.VMEM((1, GRID_V, NY), F32), dma((9,))],
        compiler_params=pltpu.CompilerParams(vmem_limit_bytes=8 << 20),
    )(*held)


def solution(mesh):
    spec = P("pos", "vel", None, None)
    return jax.shard_map(body, mesh=mesh, in_specs=(spec, spec), out_specs=(spec, spec), check_vma=False)
```

```python
import functools

import jax
import jax.numpy as jnp
from jax import lax
from jax.experimental import pallas as pl
from jax.experimental.pallas import tpu as pltpu
from jax.sharding import PartitionSpec as P

MESH = pl.DeviceIdType.MESH
COURANT = 0.4
CROWDING = 0.3
ROWS = 16
GRID_V = 64
NY = 512
TILE = 8
TILES = GRID_V // TILE
VEL = 4
POS = 32
F32 = jnp.float32
ALONG_Y = (1, 2, 3, 4)
DOWN_Y = (1, 2, 3, 4, 5)
ALONG_Z = (7, 8)
NEXT_Z = (7,)

LAST = ROWS - 2
ORDER = (7, 8, 0, ROWS - 1, 1, 2, 3, 4, 5, 6, *range(9, ROWS - 1))
LATE_ORDER = (0, ROWS - 1, 1, 2, 3, 4, 5, 6, *range(9, ROWS - 1))

FIRST = 12


def tile(t):
    return pl.ds(t * TILE, TILE)


def sublane():
    return lax.broadcasted_iota(jnp.int32, (TILE, NY), 0)


def speed_b(t):
    index = (sublane() + t * TILE).astype(F32)
    return jnp.abs(COURANT * ((index + 0.5 - GRID_V / 2) / (GRID_V / 2)))


def value_slab(c_ref, up_ref, dn_ref, x_ref, crowd, speed_x, out_ref, first=0, stop=TILES):
    place = sublane()

    def ahead(t):
        c = c_ref[tile(t), :]
        return c, pltpu.roll(c, TILE - 1, 0)

    begin = max(first - 1, 0)
    c, turned = ahead(begin)
    carried = jnp.zeros((TILE, NY), F32)
    for t in range(begin, stop):
        c_next, turned_next = ahead(t + 1) if t + 1 < TILES else (None, c)
        upper = jnp.where(place == TILE - 1, turned_next, turned) - c
        loss = pltpu.roll(upper * (1.2 + jnp.maximum(upper, 0.0)), 1, 0)
        if t >= first:
            gain = upper * (1.2 - jnp.minimum(upper, 0.0)) - jnp.where(place == 0, carried, loss)
            a_upper = up_ref[tile(t), :] - c
            a_lower = c - dn_ref[tile(t), :]
            gain = gain + a_upper * (1.2 - jnp.minimum(a_upper, 0.0))
            gain = gain - a_lower * (1.2 + jnp.maximum(a_lower, 0.0))
            y_next = pltpu.roll(c, 1 if t < TILES // 2 else NY - 1, 1)
            speed_y = speed_b(t)
            out = (1.0 - speed_x - speed_y) * c + speed_x * x_ref[tile(t), :] + speed_y * y_next
            out_ref[tile(t), :] = out + (0.125 * gain + crowd)
        carried = loss
        c, turned = c_next, turned_next


def density_slab(n_ref, n_up_ref, n_dn_ref, d_ref, d_up_ref, d_dn_ref, x_ref, speed_x, out_ref, first=0, stop=TILES):
    place = sublane()

    def ahead(t):
        d, n = d_ref[tile(t), :], n_ref[tile(t), :]
        return d, n, pltpu.roll(d, TILE - 1, 0), pltpu.roll(n, TILE - 1, 0)

    begin = max(first - 1, 0)
    d, n, d_turned, n_turned = ahead(begin)
    carried = jnp.zeros((TILE, NY), F32)
    for t in range(begin, stop):
        d_next, n_next, d_turned_next, n_turned_next = ahead(t + 1) if t + 1 < TILES else (None, None, d, n)
        last = place == TILE - 1
        d_beyond = jnp.where(last, d_turned_next, d_turned)
        step = n - jnp.where(last, n_turned_next, n_turned)
        flux = (jnp.maximum(step, 0.0) + 0.6) * (d - d_beyond) + step * d_beyond
        turned = pltpu.roll(flux, 1, 0)
        if t >= first:
            total = jnp.where(place == 0, carried, turned) - flux
            d_up, d_dn = d_up_ref[tile(t), :], d_dn_ref[tile(t), :]
            step = n - n_up_ref[tile(t), :]
            total = total - ((jnp.maximum(step, 0.0) + 0.6) * (d - d_up) + step * d_up)
            step = n_dn_ref[tile(t), :] - n
            total = total + ((jnp.maximum(step, 0.0) + 0.6) * (d_dn - d) + step * d)
            y_next = pltpu.roll(d, NY - 1 if t < TILES // 2 else 1, 1)
            speed_y = speed_b(t)
            out = (1.0 - speed_x - speed_y) * d + speed_y * y_next
            if x_ref is not None:
                out = out + speed_x * x_ref[tile(t), :]
            out_ref[tile(t), :] = out + 0.25 * total
        carried = turned
        d, n, d_turned, n_turned = d_next, n_next, d_turned_next, n_turned_next


def kernel(
    value, density, n, dn, v, d, hv, hd, crowd,
    mass, passing,
    load_sem, edge_send, edge_recv, mass_send, mass_recv, x_send, x_recv, pass_send, pass_recv, ready,
):
    vel, pos = lax.axis_index("vel"), lax.axis_index("pos")
    above, below = lax.rem(pos + 1, POS), lax.rem(pos + POS - 1, POS)
    low = vel < VEL // 2
    value_to = jnp.where(low, above, below)
    density_to = jnp.where(low, below, above)
    near = jnp.where(low, 0, 1)
    far = 1 - near
    has_lower, has_upper = vel > 0, vel < VEL - 1
    half = POS // 2
    place_x = lax.rem(pos, half)
    bottom, top = place_x == 0, place_x == half - 1
    at_end = jnp.logical_or(bottom, top)
    lower_top, upper_top = pos == half - 1, pos == POS - 1
    twin = lax.rem(pos + half, POS)
    other_end = jnp.where(bottom, pos + half - 1, pos - half + 1)
    high = jnp.logical_not(low)
    value_long = jnp.logical_or(jnp.logical_and(top, low), jnp.logical_and(bottom, high))
    density_long = jnp.logical_and(at_end, jnp.logical_not(value_long))
    up_1, down_1 = place_x == 3, place_x == 12
    up_2, down_2 = place_x == 7, place_x == 8
    any_1, any_2 = jnp.logical_or(up_1, down_1), jnp.logical_or(up_2, down_2)
    helper = jnp.logical_or(any_1, any_2)
    any_up = jnp.logical_or(up_1, up_2)
    reach = jnp.where(any_2, -4, 12)
    helped = jnp.where(any_up, pos + reach, pos - reach)
    helped_to = lax.rem(jnp.where(any_up, helped + 1, helped + POS - 1), POS)
    helps_value = jnp.logical_and(helper, jnp.where(any_up, low, high))
    via_z = jnp.where(bottom, pos + 12, jnp.where(top, pos - 12, jnp.where(up_1, pos + 4, pos - 4)))
    value_next_z = jnp.logical_and(any_1, helps_value)
    density_next_z = jnp.logical_and(any_1, jnp.logical_not(helps_value))

    barrier = pltpu.get_barrier_semaphore()

    def announce(**device):
        pl.semaphore_signal(barrier, inc=1, device_id=device, device_id_type=MESH)

    announce(pos=below)
    pl.when(jnp.logical_not(top))(lambda: announce(pos=above))
    for k in range(1, VEL):
        announce(vel=lax.rem(vel + k, VEL))

    @pl.when(bottom)
    def _():
        announce(pos=twin)
        announce(pos=other_end)

    pl.when(lower_top)(lambda: announce(pos=twin))
    pl.when(helper)(lambda: announce(pos=helped))
    pl.when(any_1)(lambda: announce(pos=helped_to))
    pl.when(place_x == 4)(lambda: announce(pos=pos + 3))
    pl.when(place_x == 11)(lambda: announce(pos=pos - 3))

    load_d = pltpu.make_async_copy(density, d.at[:, pl.ds(1, ROWS)], load_sem.at[0])
    load_v = pltpu.make_async_copy(value, v.at[:, pl.ds(1, ROWS)], load_sem.at[1])
    expected = jnp.where(bottom, 7, jnp.where(upper_top, 9, jnp.where(top, 8, jnp.where(helper, 6, 5))))
    pl.semaphore_wait(barrier, expected)

    def is_ready(**device):
        pl.semaphore_signal(ready, inc=1, device_id=device, device_id_type=MESH)

    @pl.when(top)
    def _():
        is_ready(pos=above)
        is_ready(pos=other_end)
        is_ready(pos=lax.rem(pos + 13, POS))

    pl.when(upper_top)(lambda: is_ready(pos=twin))
    pl.when(bottom)(lambda: is_ready(pos=lax.rem(pos + POS - 13, POS)))

    def x_copies(a):
        one = pl.ds(a, 1)
        return (
            pltpu.make_async_remote_copy(
                value.at[far, one], hv.at[one], x_send.at[0, a], x_recv.at[0, a],
                device_id={"pos": value_to}, device_id_type=MESH),
            pltpu.make_async_remote_copy(
                density.at[near, one], hd.at[one], x_send.at[1, a], x_recv.at[1, a],
                device_id={"pos": density_to}, device_id_type=MESH),
        )

    def x_halves(half):
        part = pl.ds(half * (GRID_V // 2), GRID_V // 2)
        return [
            pltpu.make_async_remote_copy(
                source.at[row, LAST, part], target.at[LAST, part], x_send.at[kind, LAST + 2 * half],
                x_recv.at[kind, LAST + 2 * half], device_id={"pos": to}, device_id_type=MESH)
            for kind, (source, row, target, to) in enumerate(
                ((value, far, hv, value_to), (density, near, hd, density_to)))
        ]

    def copies_of(a):
        return x_halves(0) + x_halves(1) if a == LAST else x_copies(a)

    def first_leg(kind, a, to):
        source = (value.at[far], density.at[near])[kind]
        return pltpu.make_async_remote_copy(
            source.at[pl.ds(a, 1)], passing.at[pl.ds(a - 1, 1)], x_send.at[kind, a], pass_recv.at[a - 1],
            device_id={"pos": to}, device_id_type=MESH)

    def second_leg(kind, a, to):
        return pltpu.make_async_remote_copy(
            passing.at[pl.ds(a - 1, 1)], (hv, hd)[kind].at[pl.ds(a, 1)], pass_send.at[a - 1], x_recv.at[kind, a],
            device_id={"pos": to}, device_id_type=MESH)

    def start_crossing(kind, a, passed=ALONG_Y):
        if a in passed:
            first_leg(kind, a, other_end).start()
        else:
            for copy in copies_of(a)[kind::2]:
                copy.start()

    special = jnp.logical_or(at_end, any_1)

    def start_x(rows):
        @pl.when(jnp.logical_not(special))
        def _():
            for a in rows:
                for copy in copies_of(a):
                    copy.start()

        for kind, (crosses, turns) in enumerate(((value_long, value_next_z), (density_long, density_next_z))):
            @pl.when(jnp.logical_and(special, jnp.logical_not(jnp.logical_or(crosses, turns))))
            def _():
                for a in rows:
                    for copy in copies_of(a)[kind::2]:
                        copy.start()

            @pl.when(turns)
            def _():
                for a in rows:
                    if a in NEXT_Z:
                        first_leg(kind, a, via_z).start()
                    else:
                        for copy in copies_of(a)[kind::2]:
                            copy.start()

            @pl.when(crosses)
            def _():
                for a in rows:
                    if a in ALONG_Z:
                        first_leg(kind, a, via_z).start()

            @pl.when(jnp.logical_and(crosses, top))
            def _():
                for a in rows:
                    if a not in ALONG_Z:
                        start_crossing(kind, a)

    def start_x_late():
        for kind, crosses in enumerate((value_long, density_long)):
            @pl.when(jnp.logical_and(crosses, bottom))
            def _():
                for a in LATE_ORDER:
                    start_crossing(kind, a, DOWN_Y)

    def pass_on(a, where=at_end):
        @pl.when(where)
        def _():
            first_leg(0, a, other_end).wait_recv()
            pl.when(density_long)(lambda: second_leg(0, a, twin).start())
            pl.when(value_long)(lambda: second_leg(1, a, twin).start())

    def helps_with(a):
        return helper if a in NEXT_Z else any_1

    def help_on(a):
        @pl.when(helps_with(a))
        def _():
            first_leg(0, a, helped).wait_recv()
            pl.when(helps_value)(lambda: second_leg(0, a, helped_to).start())
            pl.when(jnp.logical_not(helps_value))(lambda: second_leg(1, a, helped_to).start())

    def edge_copies(k, source, target):
        to_upper = pltpu.make_async_remote_copy(
            source.at[:, pl.ds(ROWS - 1, 1)], target.at[:, pl.ds(0, 1)], edge_send.at[k, 0], edge_recv.at[k, 0],
            device_id={"vel": lax.rem(vel + 1, VEL)}, device_id_type=MESH)
        to_lower = pltpu.make_async_remote_copy(
            source.at[:, pl.ds(0, 1)], target.at[:, pl.ds(ROWS + 1, 1)], edge_send.at[k, 1], edge_recv.at[k, 1],
            device_id={"vel": lax.rem(vel + VEL - 1, VEL)}, device_id_type=MESH)
        return to_upper, to_lower

    def start_pair(pair):
        to_upper, to_lower = pair

        @pl.when(has_upper)
        def _():
            to_upper.start()

        @pl.when(has_lower)
        def _():
            to_lower.start()

    def receive_pair(pair):
        to_upper, to_lower = pair

        @pl.when(has_lower)
        def _():
            to_upper.wait_recv()

        @pl.when(has_upper)
        def _():
            to_lower.wait_recv()

    def sent_pair(pair):
        to_upper, to_lower = pair

        @pl.when(has_upper)
        def _():
            to_upper.wait_send()

        @pl.when(has_lower)
        def _():
            to_lower.wait_send()

    edges_v, edges_d = edge_copies(0, value, v), edge_copies(1, density, d)
    start_x(ORDER[:2])
    start_pair(edges_v)
    load_d.start()
    load_v.start()
    start_x(ORDER[2:3])
    start_pair(edges_d)
    start_x(ORDER[3:FIRST])

    load_d.wait()
    place = sublane()

    def add_row(i, sums):
        parts = []
        for r in range(2):
            total = sums[r]
            for t in range(TILES):
                total = total + d[r, i + 1, tile(t), :]
            parts.append(total)
        return tuple(parts)

    zero = jnp.zeros((TILE, NY), F32)
    sums = lax.fori_loop(0, ROWS, add_row, (zero, zero))
    sums = [jnp.sum(s, axis=0, keepdims=True) for s in sums]
    mass[vel] = jnp.where(place == 0, sums[0], sums[1])
    mass_copies = [
        pltpu.make_async_remote_copy(
            mass.at[vel], mass.at[vel], mass_send.at[k], mass_recv.at[k],
            device_id={"vel": lax.rem(vel + k, VEL)}, device_id_type=MESH)
        for k in range(1, VEL)
    ]
    for copy in mass_copies:
        copy.start()
    pl.when(bottom)(lambda: pl.semaphore_wait(ready, 2))
    start_x_late()
    load_v.wait()

    def repeat_edges(field, rows):
        @pl.when(jnp.logical_not(has_lower))
        def _():
            for r in rows:
                field[r, 0] = field[r, 1]

        @pl.when(jnp.logical_not(has_upper))
        def _():
            for r in rows:
                field[r, ROWS + 1] = field[r, ROWS]

    repeat_edges(v, (0, 1))
    repeat_edges(d, (0, 1))
    for copy in mass_copies:
        copy.wait_recv()
    total = (mass[0] + mass[1]) + (mass[2] + mass[3])
    total = total / (GRID_V * GRID_V)
    total = CROWDING * total * total
    crowd[0] = jnp.broadcast_to(total[0:1], (TILE, NY))
    crowd[1] = jnp.broadcast_to(total[1:2], (TILE, NY))

    def speed_a(a):
        index = (vel * ROWS + a).astype(F32)
        return jnp.abs(COURANT * ((index + 0.5 - GRID_V / 2) / (GRID_V / 2)))

    def value_row(row, a, x_ref, **tiles):
        value_slab(v.at[row, a + 1], v.at[row, a + 2], v.at[row, a], x_ref, crowd[row], speed_a(a), n.at[row, a + 1], **tiles)

    def density_row(row, a, x_ref, out_ref, **tiles):
        density_slab(
            n.at[row, a + 1], n.at[row, a + 2], n.at[row, a],
            d.at[row, a + 1], d.at[row, a + 2], d.at[row, a], x_ref, speed_a(a), out_ref, **tiles)

    def arrive(a):
        for copy in x_copies(a):
            copy.wait_recv()

    def finish_far(a, first=0, stop=TILES):
        speed_x = speed_a(a)
        for t in range(first, stop):
            dn[far, a, tile(t), :] = dn[far, a, tile(t), :] + speed_x * hd[a, tile(t), :]

    def near_density(a, **tiles):
        density_row(near, a, d.at[far, a + 1], dn.at[near, a], **tiles)

    def inner_values(here):
        @pl.loop(jnp.where(here, 1, ROWS - 1), ROWS - 1)
        def _(a):
            value_row(far, a, v.at[near, a + 1])

    inner_values(at_end)

    receive_pair(edges_v)

    @pl.loop(0, 2)
    def _(i):
        a = i * (ROWS - 1)
        arrive(a)
        value_row(far, a, v.at[near, a + 1])
        value_row(near, a, hv.at[a])

    edges_n = edge_copies(2, n.at[:, pl.ds(1, ROWS)], n)
    start_pair(edges_n)
    repeat_edges(n, (0, 1))
    inner_values(jnp.logical_not(at_end))
    pl.when(jnp.logical_or(lower_top, any_1))(lambda: pl.semaphore_wait(ready, 1))
    for a in ALONG_Z:
        help_on(a)
    start_x(ORDER[FIRST:])
    pass_on(1)
    pass_on(2)
    pass_on(3)

    @pl.loop(1, ROWS - 1)
    def _(a):
        density_row(far, a, None, dn.at[far, a])

    receive_pair(edges_d)


    def near_step(a):
        arrive(a)
        value_row(near, a, hv.at[a])
        finish_far(a)

    @pl.loop(1, ROWS // 2)
    def _(a):
        pl.when(a + 3 <= ALONG_Y[-1])(lambda: pass_on(a + 3))
        pl.when(a + 3 == DOWN_Y[-1])(lambda: pass_on(a + 3, top))
        near_step(a)

        @pl.when(a > 1)
        def _():
            near_density(a - 1)

    receive_pair(edges_n)

    @pl.loop(0, 2)
    def _(i):
        a = i * (ROWS - 1)
        density_row(far, a, None, dn.at[far, a])
        finish_far(a)

    near_density(0)

    @pl.loop(ROWS // 2, LAST)
    def _(a):
        near_step(a)
        near_density(a - 1)

    for copy in x_halves(0) + x_halves(1):
        copy.wait_recv()

    for pair in (edges_v, edges_d, edges_n):
        sent_pair(pair)
    for copy in mass_copies:
        copy.wait_send()

    @pl.loop(0, LAST)
    def _(a):
        for copy in x_copies(a):
            copy.wait_send()

    for copy in x_copies(ROWS - 1) + tuple(x_halves(0) + x_halves(1)):
        copy.wait_send()

    @pl.when(at_end)
    def _():
        for a in ALONG_Y:
            second_leg(0, a, twin).wait_send()

    pl.when(top)(lambda: second_leg(0, DOWN_Y[-1], twin).wait_send())

    for a in ALONG_Z:
        pl.when(helps_with(a))(lambda: second_leg(0, a, helped_to).wait_send())


def store(n, dn, v, d, hv, hd, crowd, value_out, density_out, last_value, last_density, last_far, sem):
    vel = lax.axis_index("vel")
    near = jnp.where(vel < VEL // 2, 0, 1)
    far = 1 - near
    count = [0]

    def copy(source, target):
        made = pltpu.make_async_copy(source, target, sem.at[count[0]])
        count[0] += 1
        made.start()
        return made

    def rows(first, stop):
        return pl.ds(first, stop - first)

    copies = [
        copy(n.at[far, rows(1, ROWS + 1)], value_out.at[far]),
        copy(n.at[near, rows(1, LAST + 1)], value_out.at[near, rows(0, LAST)]),
        copy(dn.at[far, rows(0, LAST)], density_out.at[far, rows(0, LAST)]),
        copy(dn.at[near, rows(0, LAST - 1)], density_out.at[near, rows(0, LAST - 1)]),
        copy(n.at[near, rows(LAST + 2, ROWS + 1)], value_out.at[near, rows(LAST + 1, ROWS)]),
        copy(dn.at[far, rows(LAST + 1, ROWS)], density_out.at[far, rows(LAST + 1, ROWS)]),
    ]

    def speed(a):
        index = (vel * ROWS + a).astype(F32)
        return jnp.abs(COURANT * ((index + 0.5 - GRID_V / 2) / (GRID_V / 2)))

    for t in range(TILES):
        last_far[0, tile(t), :] = dn[far, LAST, tile(t), :] + speed(LAST) * hd[LAST, tile(t), :]
    copies.append(copy(last_far, density_out.at[far, rows(LAST, LAST + 1)]))
    at = LAST + 1
    value_slab(
        v.at[near, at], v.at[near, at + 1], v.at[near, at - 1], hv.at[LAST], crowd[near], speed(LAST), last_value.at[0])
    copies.append(copy(last_value, value_out.at[near, rows(LAST, LAST + 1)]))
    levels = [n.at[near, at - 2], n.at[near, at - 1], last_value.at[0], n.at[near, at + 1], n.at[near, at + 2]]
    for k in range(3):
        here = at - 1 + k
        density_slab(
            levels[k + 1], levels[k + 2], levels[k], d.at[near, here], d.at[near, here + 1], d.at[near, here - 1],
            d.at[far, here], speed(here - 1), last_density.at[k])
    copies.append(copy(last_density, density_out.at[near, rows(LAST - 1, ROWS)]))
    for made in copies:
        made.wait()


def body(value_next, density):
    shape = (2, ROWS, GRID_V, NY)
    haloed = pltpu.VMEM((2, ROWS + 2, GRID_V, NY), F32)
    slab = pltpu.VMEM((ROWS, GRID_V, NY), F32)
    dma = pltpu.SemaphoreType.DMA
    held = pl.pallas_call(
        kernel,
        out_shape=[haloed, pltpu.VMEM(shape, F32), haloed, haloed, slab, slab, pltpu.VMEM((2, TILE, NY), F32)],
        in_specs=[pl.BlockSpec(memory_space=pltpu.HBM)] * 2,
        out_specs=[pl.BlockSpec(memory_space=pltpu.VMEM)] * 7,
        scratch_shapes=[
            pltpu.VMEM((VEL, TILE, NY), F32),
            pltpu.VMEM((ALONG_Z[-1], GRID_V, NY), F32),
            dma((2,)), dma((3, 2)), dma((3, 2)), dma((VEL,)), dma((VEL,)),
            dma((2, ROWS + 1)), dma((2, ROWS + 1)), dma((ALONG_Z[-1],)), dma((ALONG_Z[-1],)), pltpu.SemaphoreType.REGULAR,
        ],
        compiler_params=pltpu.CompilerParams(
            collective_id=0, has_side_effects=True, vmem_limit_bytes=40 << 20
        ),
    )(value_next, density)
    return pl.pallas_call(
        store,
        out_shape=[jax.ShapeDtypeStruct(shape, F32)] * 2,
        in_specs=[pl.BlockSpec(memory_space=pltpu.VMEM)] * 7,
        out_specs=[pl.BlockSpec(memory_space=pl.ANY)] * 2,
        scratch_shapes=[pltpu.VMEM((1, GRID_V, NY), F32), pltpu.VMEM((3, GRID_V, NY), F32), pltpu.VMEM((1, GRID_V, NY), F32), dma((9,))],
        compiler_params=pltpu.CompilerParams(vmem_limit_bytes=8 << 20),
    )(*held)


def solution(mesh):
    spec = P("pos", "vel", None, None)
    return jax.shard_map(body, mesh=mesh, in_specs=(spec, spec), out_specs=(spec, spec), check_vma=False)
```
